256 devices in a mesh: region: 4 (over x), comp: 64 (over z, y, core).
Axes of the slice: x: 4, y: 4, z: 8, core: 2. Of those that a mesh axis runs over, the one named last changes fastest.
Arguments:
- spectrum: float32 [1728, 1024, 128], P('comp', 'region'), may hold values from 0.2 to 2
- wind: float32 [2, 1024, 128], P(None, 'region'), may hold values from -6 to 6
- sea_table: int32 [256, 512], P('region'), may hold values from -1 to 32767, as said below
- transfer_kernel: bfloat16 [1728, 1728], replicated, may hold values from -0.15625 to 0.15625
Outputs:
- spectrum_out: float32 [1728, 1024, 128], P('comp', 'region')
The draws below stay inside these ranges and needn't reach their ends.
Inputs may be any that keep to these rules, and one draw needn't show every extreme that they name: `sea_table`: row r * 64 + d lists first distinct cells of block d of region r (cells d * 512 to (d + 1) * 512 - 1, numbered x' * 128 + y within the region), then -1 in its other slots; each region's rows hold, in some order, 16 rows each of 512, 256, 128 and 128 listed cells, so a region holds exactly 16384 sea cells; unlisted cells are land.
All inputs are finite; a program needn't handle non-finite values.
Results may differ from the reference program's by a relative error of at most 0.0011.
Values sent between devices are 32-bit elements; how exact they have to be, the bound alone decides.
A program may use at most 128 MiB of HBM per device.

```python
import math
import jax
import jax.numpy as jnp
from jax import lax

NDIR = 36
NFREQ = 48
NSUB = 2
GX = 256
GY = 128
SPEC = 1728
NX = 1024
BLOCK = 512
N_REGION = 4
N_COMP = 64


def draw_sea_table(key, part):
    key = jax.random.fold_in(key, 11)
    block_cells = GX * GY // N_COMP
    row_total = N_REGION * N_COMP
    pattern = jnp.array([block_cells, block_cells // 2, block_cells // 4, block_cells // 4], dtype=jnp.int32)
    pattern = jnp.tile(pattern, N_COMP // 4)
    region_keys = jax.random.split(jax.random.fold_in(key, 1), N_REGION)
    orders = jax.vmap(lambda single: jax.random.permutation(single, N_COMP))(region_keys)
    sea_counts = pattern[orders].reshape(row_total)
    row_keys = jax.random.split(jax.random.fold_in(key, 2), row_total)
    cell_orders = jax.vmap(lambda single: jax.random.permutation(single, block_cells))(row_keys)
    block_index = jnp.arange(row_total, dtype=jnp.int32) % N_COMP
    slot_index = jnp.arange(block_cells, dtype=jnp.int32)
    listed = block_index[:, None] * block_cells + cell_orders.astype(jnp.int32)
    return jnp.where(slot_index[None, :] < sea_counts[:, None], listed, -1).astype(jnp.int32)


def level_of(stream_key, shape, cuts, low, high):
    def one(dim, blocks):
        heights = jax.random.uniform(jax.random.fold_in(jax.random.fold_in(stream_key, 6), dim), (blocks,), jnp.float32, low / len(cuts), high / len(cuts))
        return jnp.repeat(jnp.exp(heights), shape[dim] // blocks).reshape((-1,) + (1,) * (len(shape) - dim - 1))

    factor_of = one(*cuts[0])
    for cut in cuts[1:]:
        factor_of = factor_of * one(*cut)
    return factor_of


def bell_draw(key, extent, scale, most, cuts=(), held_as=jnp.bfloat16):
    entries = scale * jax.random.normal(key, extent, jnp.float32)
    if cuts:
        entries = entries * level_of(key, extent, cuts, -0.22, 0.18)
    return jnp.clip(entries, -most, most).astype(held_as)


def setup_inputs(seed: int = 0) -> dict:
    key_list = jax.random.split(jax.random.key(seed), 5)
    spectrum = jnp.clip(jnp.exp(math.log(2.0) - 2.3025851 * jax.random.uniform(key_list[0], (SPEC, NX, GY), jnp.float32) ** level_of(key_list[0], (SPEC, NX, GY), ((0, 64), (1, 4)), -0.2, 0.2)), 0.2, 2.0)
    wind = bell_draw(key_list[1], (2, NX, GY), 1.5, 6.0, ((1, 4),), jnp.float32)
    sea_table = draw_sea_table(jax.random.fold_in(key_list[4], 71), 0)
    transfer_kernel = bell_draw(key_list[3], (SPEC, SPEC), SPEC ** -0.5, 0.15625)
    return dict(spectrum=spectrum, wind=wind, sea_table=sea_table, transfer_kernel=transfer_kernel)


growth_rate = 0.05
wind_floor = 0.5
dissipation = 0.02
coupling = 0.5
courant_top = 0.6
ratio_log = math.log(1.1)


def spectral_consts(first_comp, comp_total):
    comp_ids = first_comp + jnp.arange(comp_total, dtype=jnp.int32)
    freq_number = (comp_ids // NDIR).astype(jnp.float32)
    dir_number = (comp_ids % NDIR).astype(jnp.float32)
    centre = float(NFREQ // 2)
    all_freqs = jnp.arange(NFREQ, dtype=jnp.int32).astype(jnp.float32)
    normaliser = NDIR * jnp.sum(jnp.exp((all_freqs - centre) * ratio_log))
    frequency = jnp.exp((freq_number - centre) * ratio_log)
    direction = 2.0 * math.pi * (dir_number + 0.5) / NDIR
    group_speed = courant_top * jnp.exp(-freq_number * ratio_log)
    return frequency, jnp.cos(direction), jnp.sin(direction), group_speed, frequency / normaliser


def upwind(wave_field, padded, sea_mask, velocity_x, velocity_y):
    west_side = padded[..., :-2, :]
    east_side = padded[..., 2:, :]
    widths = [(0, 0)] * (wave_field.ndim - 1) + [(1, 1)]
    y_padded = jnp.pad(wave_field, widths)
    south_side = y_padded[..., :-2]
    north_side = y_padded[..., 2:]
    plus_x = jnp.maximum(velocity_x, 0.0)
    minus_x = jnp.minimum(velocity_x, 0.0)
    plus_y = jnp.maximum(velocity_y, 0.0)
    minus_y = jnp.minimum(velocity_y, 0.0)
    changed = (wave_field - plus_x * (wave_field - west_side) - minus_x * (east_side - wave_field)
               - plus_y * (wave_field - south_side) - minus_y * (north_side - wave_field))
    return sea_mask * changed


def source_update(points, wind_points, kernel, consts):
    frequency, cosine_dir, sine_dir, group_speed, weights = consts
    energy = jnp.sum(weights[:, None] * points, axis=0)
    projection = cosine_dir[:, None] * wind_points[0][None, :] + sine_dir[:, None] * wind_points[1][None, :]
    growth = growth_rate * frequency[:, None] * jnp.maximum(projection - wind_floor, 0.0)
    damping = -dissipation * (frequency * frequency)[:, None] * (energy * energy)[None, :]
    rounded = lax.optimization_barrier(points.astype(jnp.bfloat16)).astype(jnp.float32)
    coupled = jnp.dot(kernel.astype(jnp.float32), rounded, precision=lax.Precision.HIGHEST,
                      preferred_element_type=jnp.float32)
    change = (growth + damping) * points + coupling * points * coupled
    return points + change / (1.0 - damping)


def reference(spectrum, wind, sea_table, transfer_kernel):
    cell_count = GX * GY
    listed = sea_table.reshape(N_REGION, N_COMP * BLOCK)
    region_base = (jnp.arange(N_REGION, dtype=jnp.int32) * cell_count)[:, None]
    flat_ids = jnp.where(listed >= 0, listed + region_base, N_REGION * cell_count).reshape(-1)
    sea_mask = jnp.zeros((N_REGION * cell_count,), jnp.float32).at[flat_ids].set(1.0, mode="drop")
    sea_mask = sea_mask.reshape(NX, GY)
    masked = sea_mask[None] * spectrum
    slabs = masked.reshape(NFREQ, NDIR, NX, GY)

    def propagate(inputs):
        freq_slab, freq_number = inputs
        frequency, cosine_dir, sine_dir, group_speed, weights = spectral_consts(freq_number * NDIR, NDIR)
        velocity_x = (group_speed * cosine_dir)[:, None, None]
        velocity_y = (group_speed * sine_dir)[:, None, None]
        for substep in range(NSUB):
            padded = jnp.pad(freq_slab, ((0, 0), (1, 1), (0, 0)))
            freq_slab = upwind(freq_slab, padded, sea_mask, velocity_x, velocity_y)
        return freq_slab

    propagated = lax.map(propagate, (slabs, jnp.arange(NFREQ, dtype=jnp.int32)))
    propagated = propagated.reshape(SPEC, NX * GY)
    wind_flat = wind.reshape(2, NX * GY)
    consts = spectral_consts(0, SPEC)

    def column_block(block_number):
        first_column = block_number * BLOCK
        points = lax.dynamic_slice_in_dim(propagated, first_column, BLOCK, 1)
        wind_points = lax.dynamic_slice_in_dim(wind_flat, first_column, BLOCK, 1)
        return source_update(points, wind_points, transfer_kernel, consts)

    updated = lax.map(column_block, jnp.arange(N_REGION * N_COMP, dtype=jnp.int32))
    return jnp.transpose(updated, (1, 0, 2)).reshape(SPEC, NX, GY)
```

```python
import functools
import math

import jax
import jax.numpy as jnp
import numpy as np
from jax import lax
from jax.experimental import pallas as pl
from jax.experimental.pallas import tpu as pltpu
from jax.sharding import PartitionSpec as P

NDIR = 36
NFREQ = 48
SPEC = NDIR * NFREQ
COMPS = 64
LOCAL = SPEC // COMPS
REGIONS = 4
ROWS = 256
LANES = 128
UNITS = 128
BLOCKS = 64
PADDED_ROWS = ROWS + 8
PADDED_COMP = 32
PADDED_SPEC = SPEC + 32
TILE = 432
F32 = jnp.float32
MESH = pl.DeviceIdType.MESH

growth_rate = 0.05
wind_floor = 0.5
dissipation = 0.02
coupling = 0.5
courant_top = 0.6


def component_table():
    comp = np.arange(SPEC)
    freq, direction = comp // NDIR, 2.0 * math.pi * (comp % NDIR + 0.5) / NDIR
    omega = 1.1 ** (freq - NFREQ // 2)
    speed = courant_top * 1.1 ** (-freq.astype(np.float64))
    cosine, sine = np.cos(direction), np.sin(direction)
    u, v = speed * cosine, speed * sine
    centre = 1.0 - np.abs(u) - np.abs(v)
    columns = [omega, cosine, sine, centre, np.maximum(u, 0), np.maximum(-u, 0), np.maximum(v, 0), np.maximum(-v, 0)]
    table = np.zeros((SPEC, LANES), np.float32)
    for lane, column in enumerate(columns):
        table[:, lane] = column
    return table.reshape(COMPS, LOCAL, LANES)


def energy_scale():
    return float(1.0 / (NDIR * np.sum(1.1 ** (np.arange(NFREQ) - NFREQ // 2.0))))


def shifted(me, step):
    z = (me // 8 + step // 8) % 8
    y = ((me // 2) % 4 + (step // 2) % 4) % 4
    core = (me % 2 + step % 2) % 2
    return z * 8 + y * 2 + core


def gathered(source, lanes):
    return jnp.take_along_axis(source, lanes, axis=1, mode="promise_in_bounds")


def exchange_kernel(
    spectrum, wind_field, sea_table, transfer, table,
    compact, lane_map, part_map, unit_rows,
    natural, wind, wave0, wave1, wave2, mask, sea_rows, units_smem,
    kernel_buf, constants, own, omega, cosine, sine,
    outgoing, incoming, dense, rounded, coupled, returning,
    load_sem, halo_send, halo_recv, send_sem, forward_sem, back_sem, self_sem,
):
    me = lax.axis_index("comp")
    region = lax.axis_index("region")
    west = (region + REGIONS - 1) % REGIONS
    east = (region + 1) % REGIONS

    load_spectrum = pltpu.make_async_copy(spectrum, natural.at[pl.ds(0, LOCAL * ROWS)], load_sem.at[0])
    load_spectrum.start()
    load_own = pltpu.make_async_copy(table.at[me], own, load_sem.at[1])
    load_own.start()
    load_constants = pltpu.make_async_copy(table, constants, load_sem.at[2])
    load_constants.start()
    load_kernel = pltpu.make_async_copy(transfer, kernel_buf, load_sem.at[3])
    load_kernel.start()

    load_wind = pltpu.make_async_copy(wind_field, wind.at[pl.ds(0, 2 * ROWS)], load_sem.at[5])
    load_wind.start()

    barrier = pltpu.get_barrier_semaphore()

    @pl.loop(1, COMPS)
    def _(step):
        pl.semaphore_signal(barrier, inc=1, device_id={"comp": shifted(me, step)}, device_id_type=MESH)

    pl.semaphore_signal(barrier, inc=1, device_id={"region": west}, device_id_type=MESH)
    pl.semaphore_signal(barrier, inc=1, device_id={"region": east}, device_id_type=MESH)

    for part in range(4):
        sea_rows[pl.ds(part, BLOCKS, stride=4), :] = sea_table[:, part * LANES : (part + 1) * LANES]

    listed = sea_rows[0:ROWS, :] >= 0
    held = jnp.where(listed, 1.0, 0.0).astype(jnp.bfloat16)
    lower = jnp.where(
        lax.broadcasted_iota(jnp.int32, (ROWS, ROWS), 0) > lax.broadcasted_iota(jnp.int32, (ROWS, ROWS), 1), 1.0, 0.0
    ).astype(jnp.bfloat16)
    rank = jnp.dot(lower, held, preferred_element_type=F32)
    unit = lax.broadcasted_iota(jnp.int32, (ROWS, UNITS), 1).astype(F32)
    row_number = lax.broadcasted_iota(jnp.int32, (ROWS, UNITS), 0).astype(F32)
    found = jnp.where((rank == unit) & listed, row_number, 0.0)
    unit_rows[...] = jnp.broadcast_to(jnp.sum(found, axis=0, keepdims=True), (8, UNITS)).astype(jnp.int32)
    load_units = pltpu.make_async_copy(unit_rows, units_smem, load_sem.at[4])
    load_units.start()

    lane_number = lax.broadcasted_iota(jnp.int32, (LANES, 4 * LANES), 0)
    slot = lax.broadcasted_iota(jnp.int32, (1, 4 * LANES), 1)
    slot_lane = (slot % LANES).astype(F32)
    slot_part = (slot // LANES).astype(F32)
    quarter = lax.broadcasted_iota(jnp.int32, (8, 4 * LANES), 0)

    @pl.loop(0, BLOCKS, unroll=8)
    def _(block):
        cells = sea_table[pl.ds(block, 1), :]
        lane = jnp.where(cells >= 0, cells % LANES, -1)
        inside = jnp.where(cells >= 0, (cells // LANES) % 4, -1)
        match = jnp.where(lane == lane_number, 1.0, 0.0).astype(jnp.bfloat16)
        row = jnp.where(inside == quarter, 1.0, 0.0)
        rows = jnp.concatenate([row, row * slot_lane, row * slot_part], axis=0).astype(jnp.bfloat16)
        maps = lax.dot_general(rows, match, (((1,), (1,)), ((), ())), preferred_element_type=F32)
        target = pl.ds(pl.multiple_of(block * 4, 4), 4)
        present = maps[0:4]
        mask[target, :] = present
        lane_map[target, :] = maps[8:12].astype(jnp.int32)
        part_map[target, :] = jnp.where(present > 0.5, maps[16:20], -1.0).astype(jnp.int32)

    load_own.wait()
    coefficients = own[...]
    lanes = lax.broadcasted_iota(jnp.int32, (LOCAL, LANES), 1)

    def column(number):
        return jnp.broadcast_to(coefficients[:, number : number + 1], (LOCAL, LANES))

    centre_w, west_w, east_w = column(3), column(4), column(5)
    south_w = jnp.where(lanes == 0, 0.0, column(6))
    north_w = jnp.where(lanes == LANES - 1, 0.0, column(7))

    def mask_row(x):
        return jnp.broadcast_to(mask[pl.ds(x, 1), :], (LOCAL, LANES))

    def first(x):
        wave0[x + 1] = mask_row(x) * natural[pl.ds(x, LOCAL, stride=ROWS), :]

    def substep(source, target, shift, x):
        here = source[x + 1]
        changed = (
            centre_w * here
            + west_w * source[x]
            + east_w * source[x + 2]
            + south_w * pltpu.roll(here, 1, 1)
            + north_w * pltpu.roll(here, LANES - 1, 1)
        )
        target[x + shift] = mask_row(x) * changed

    def halo(wave, number):
        to_west = pltpu.make_async_remote_copy(
            wave.at[1], wave.at[ROWS + 1], halo_send.at[2 * number], halo_recv.at[2 * number],
            device_id={"region": west}, device_id_type=MESH)
        to_east = pltpu.make_async_remote_copy(
            wave.at[ROWS], wave.at[0], halo_send.at[2 * number + 1], halo_recv.at[2 * number + 1],
            device_id={"region": east}, device_id_type=MESH)
        to_west.start()
        to_east.start()
        return to_west, to_east

    def arrived(wave, copies):
        for copy in copies:
            copy.wait()
        wave[0] = jnp.where(region > 0, wave[0], 0.0)
        wave[ROWS + 1] = jnp.where(region < REGIONS - 1, wave[ROWS + 1], 0.0)

    load_spectrum.wait()
    first(0)
    first(ROWS - 1)
    pl.semaphore_wait(barrier, COMPS + 1)
    copies = halo(wave0, 0)

    @pl.loop(1, ROWS - 1, unroll=8)
    def _(x):
        first(x)

    @pl.loop(1, ROWS - 1, unroll=8)
    def _(x):
        substep(wave0, wave1, 1, x)

    arrived(wave0, copies)
    substep(wave0, wave1, 1, 0)
    substep(wave0, wave1, 1, ROWS - 1)
    copies = halo(wave1, 1)

    @pl.loop(1, ROWS - 1, unroll=8)
    def _(x):
        substep(wave1, wave2, 0, x)

    arrived(wave1, copies)
    substep(wave1, wave2, 0, 0)
    substep(wave1, wave2, 0, ROWS - 1)

    load_units.wait()

    def unit_cells(number):
        row = jnp.clip(units_smem[0, number], 0, ROWS - 1)
        cells = sea_rows[pl.ds(row, 1), :]
        return row & ~3, cells & (LANES - 1), (cells >> 7) & 3

    def packed(number):
        base, lane, inside = unit_cells(number)
        lane = jnp.broadcast_to(lane, (LOCAL, LANES))
        inside = jnp.broadcast_to(inside, (LOCAL, LANES))
        total = gathered(wave2[base], lane)
        for quarter in range(1, 4):
            total = jnp.where(inside == quarter, gathered(wave2[base + quarter], lane), total)
        return total

    def forward(chunk, target):
        return pltpu.make_async_remote_copy(
            outgoing.at[2 * target + chunk], incoming.at[chunk, me], send_sem.at[0], forward_sem.at[chunk, me],
            device_id={"comp": target}, device_id_type=MESH)

    for chunk in range(2):

        @pl.loop(1, COMPS)
        def _(step, chunk=chunk):
            target = shifted(me, step)
            outgoing[2 * target + chunk] = packed(2 * target + chunk)
            forward(chunk, target).start()

    for chunk in range(2):
        incoming[chunk, me] = packed(2 * me + chunk)

    load_constants.wait()

    @pl.loop(0, COMPS, unroll=4)
    def _(source):
        values = constants[source]
        omega[source] = jnp.broadcast_to(values[:, 0:1], (LOCAL, LANES))
        cosine[source] = jnp.broadcast_to(values[:, 1:2], (LOCAL, LANES))
        sine[source] = jnp.broadcast_to(values[:, 2:3], (LOCAL, LANES))

    load_kernel.wait()
    load_wind.wait()

    def wind_at(chunk):
        base, lane, inside = unit_cells(2 * me + chunk)
        lane = jnp.broadcast_to(lane, (8, LANES))
        parts = []
        for part in range(2):
            total = jnp.zeros((8, LANES), F32)
            for quarter in range(4):
                line = jnp.broadcast_to(wind[pl.ds(part * ROWS + base + quarter, 1), :], (8, LANES))
                total = jnp.where(inside == quarter, gathered(line, lane), total)
            parts.append(total[0:1])
        return parts

    def back(chunk, target):
        return pltpu.make_async_remote_copy(
            returning.at[chunk, target], compact.at[2 * me + chunk], send_sem.at[1], back_sem.at[chunk, me],
            device_id={"comp": target}, device_id_type=MESH)

    for chunk in range(2):

        @pl.loop(1, COMPS)
        def _(step, chunk=chunk):
            source = shifted(me, step)
            pltpu.make_async_remote_copy(
                outgoing.at[0], incoming.at[chunk, source], send_sem.at[0], forward_sem.at[chunk, source],
                device_id={"comp": source}, device_id_type=MESH).wait_recv()

        wind_u, wind_v = wind_at(chunk)

        def collect(source, total, chunk=chunk):
            values = incoming[chunk, source]
            dense[pl.ds(source * LOCAL, LOCAL), :] = values
            return total + omega[source] * values

        total = lax.fori_loop(0, COMPS, collect, jnp.zeros((LOCAL, LANES), F32), unroll=True)
        energy = jnp.sum(total, axis=0, keepdims=True) * energy_scale()
        loss = dissipation * energy * energy
        rounded[...] = dense[0:SPEC, :].astype(jnp.bfloat16)

        @pl.loop(0, SPEC // TILE)
        def _(tile):
            rows = pl.ds(pl.multiple_of(tile * TILE, TILE), TILE)
            coupled[rows, :] = jnp.dot(kernel_buf[rows, :], rounded[...], preferred_element_type=F32)

        def updated(target, chunk=chunk, wind_u=wind_u, wind_v=wind_v, loss=loss):
            points = incoming[chunk, target]
            speed = omega[target]
            along = cosine[target] * wind_u + sine[target] * wind_v
            growth = growth_rate * speed * jnp.maximum(along - wind_floor, 0.0)
            damping = speed * speed * loss
            joined = coupled[pl.ds(target * LOCAL, LOCAL), :]
            return points + points * (growth - damping + coupling * joined) / (1.0 + damping)

        @pl.loop(1, COMPS)
        def _(step, chunk=chunk, updated=updated):
            target = shifted(me, step)
            returning[chunk, target] = updated(target)
            back(chunk, target).start()

        returning[chunk, me] = updated(me)
        pltpu.make_async_copy(returning.at[chunk, me], compact.at[2 * me + chunk], self_sem.at[chunk]).start()

    for chunk in range(2):

        @pl.loop(1, COMPS)
        def _(step, chunk=chunk):
            source = shifted(me, step)
            pltpu.make_async_remote_copy(
                returning.at[chunk, source], compact.at[2 * source + chunk], send_sem.at[1], back_sem.at[chunk, source],
                device_id={"comp": source}, device_id_type=MESH).wait_recv()

        pltpu.make_async_copy(returning.at[chunk, me], compact.at[2 * me + chunk], self_sem.at[chunk]).wait()

    for number in range(2):
        sent = outgoing.at[pl.ds(0, 2 * COMPS - 2)]
        pltpu.make_async_copy(sent, sent, send_sem.at[number]).wait()


def expand_kernel(compact, lane_map, part_map, units, result, spread, store_sem):
    @pl.loop(0, UNITS // 4)
    def _(group):
        pieces = []
        for offset in range(4):
            number = group * 4 + offset
            row = jnp.clip(units[0, number], 0, ROWS - 1)
            base, part = row & ~3, row & 3
            slots = compact[number]
            for quarter in range(4):
                line = pl.ds(base + quarter, 1)
                lane = jnp.broadcast_to(lane_map[line, :], (LOCAL, LANES))
                here = jnp.broadcast_to(part_map[line, :], (LOCAL, LANES)) == part
                pieces.append((base + quarter, part, here, gathered(slots, lane)))
        for line, part, here, values in pieces:
            target = pl.ds(line, LOCAL, stride=ROWS)
            before = jnp.where(part == 0, 0.0, spread[target, :])
            spread[target, :] = jnp.where(here, values, before)

    store = pltpu.make_async_copy(spread.at[pl.ds(0, LOCAL * ROWS)], result, store_sem)
    store.start()
    store.wait()


def on_device(spectrum, wind, sea_table, transfer_kernel):
    table = jnp.asarray(component_table())
    vmem = pl.BlockSpec(memory_space=pltpu.VMEM)
    anywhere = pl.BlockSpec(memory_space=pl.ANY)
    wave = pltpu.VMEM((ROWS + 2, LOCAL, LANES), F32)
    per_source = pltpu.VMEM((COMPS, LOCAL, LANES), F32)
    dma = pltpu.SemaphoreType.DMA
    shape = jax.ShapeDtypeStruct
    compact, lane_map, part_map, unit_rows = pl.pallas_call(
        exchange_kernel,
        out_shape=(
            shape((UNITS, LOCAL, LANES), F32),
            shape((PADDED_ROWS, LANES), jnp.int32),
            shape((PADDED_ROWS, LANES), jnp.int32),
            shape((8, UNITS), jnp.int32),
        ),
        in_specs=[anywhere, anywhere, vmem, anywhere, anywhere],
        out_specs=(anywhere, vmem, vmem, vmem),
        scratch_shapes=[
            pltpu.VMEM((PADDED_COMP * ROWS, LANES), F32),
            pltpu.VMEM((2 * ROWS + 8, LANES), F32),
            wave,
            wave,
            pltpu.VMEM((ROWS, LOCAL, LANES), F32),
            pltpu.VMEM((PADDED_ROWS, LANES), F32),
            pltpu.VMEM((PADDED_ROWS, LANES), jnp.int32),
            pltpu.SMEM((8, UNITS), jnp.int32),
            pltpu.VMEM((SPEC, SPEC), jnp.bfloat16),
            per_source,
            pltpu.VMEM((LOCAL, LANES), F32),
            per_source,
            per_source,
            per_source,
            pltpu.VMEM((UNITS, LOCAL, LANES), F32),
            pltpu.VMEM((2, COMPS, LOCAL, LANES), F32),
            pltpu.VMEM((PADDED_SPEC, LANES), F32),
            pltpu.VMEM((SPEC, LANES), jnp.bfloat16),
            pltpu.VMEM((PADDED_SPEC, LANES), F32),
            pltpu.VMEM((2, COMPS, LOCAL, LANES), F32),
            dma((6,)),
            dma((4,)),
            dma((4,)),
            dma((2,)),
            dma((2, COMPS)),
            dma((2, COMPS)),
            dma((2,)),
        ],
        compiler_params=pltpu.CompilerParams(
            collective_id=0, has_side_effects=True, vmem_limit_bytes=56 * 1024 * 1024
        ),
        cost_estimate=pl.CostEstimate(flops=2 * SPEC * SPEC * 256, bytes_accessed=16 << 20, transcendentals=0),
        name="exchange",
    )(spectrum.reshape(LOCAL * ROWS, LANES), wind.reshape(2 * ROWS, LANES), sea_table, transfer_kernel, table)
    result = pl.pallas_call(
        expand_kernel,
        out_shape=shape((LOCAL * ROWS, LANES), F32),
        in_specs=[vmem, vmem, vmem, pl.BlockSpec(memory_space=pltpu.SMEM)],
        out_specs=anywhere,
        scratch_shapes=[pltpu.VMEM((PADDED_COMP * ROWS, LANES), F32), dma],
        compiler_params=pltpu.CompilerParams(vmem_limit_bytes=32 * 1024 * 1024),
        cost_estimate=pl.CostEstimate(flops=1 << 20, bytes_accessed=6 << 20, transcendentals=0),
        name="expand",
    )(compact, lane_map, part_map, unit_rows)
    return result.reshape(LOCAL, ROWS, LANES)


def solution(mesh):
    placed = (P("comp", "region", None), P(None, "region", None), P("region", None), P())
    return jax.shard_map(
        on_device, mesh=mesh, in_specs=placed, out_specs=P("comp", "region", None), check_vma=False
    )
```

```python
import math

import jax
import jax.numpy as jnp
import numpy as np
from jax import lax
from jax.experimental import pallas as pl
from jax.experimental.pallas import tpu as pltpu
from jax.sharding import PartitionSpec as P

NDIR = 36
NFREQ = 48
SPEC = NDIR * NFREQ
COMPS = 64
LOCAL = SPEC // COMPS
REGIONS = 4
ROWS = 256
LANES = 128
BLOCKS = 64
STRIDE = ROWS + 16
PADDED_ROWS = ROWS + 8
PADDED_COMP = 32
PADDED_SPEC = SPEC + 32
TILE = 432
F32 = jnp.float32
MESH = pl.DeviceIdType.MESH

growth_rate = 0.05
wind_floor = 0.5
dissipation = 0.02
coupling = 0.5
courant_top = 0.6


def component_tables():
    comp = np.arange(SPEC)
    freq, direction = comp // NDIR, 2.0 * math.pi * (comp % NDIR + 0.5) / NDIR
    omega = 1.1 ** (freq - NFREQ // 2)
    speed = courant_top * 1.1 ** (-freq.astype(np.float64))
    cosine, sine = np.cos(direction), np.sin(direction)
    u, v = speed * cosine, speed * sine
    centre = 1.0 - np.abs(u) - np.abs(v)
    columns = [omega, cosine, sine, centre, np.maximum(u, 0), np.maximum(-u, 0), np.maximum(v, 0), np.maximum(-v, 0)]
    table = np.zeros((SPEC, LANES), np.float32)
    for lane, column in enumerate(columns):
        table[:, lane] = column
    scalars = np.zeros((COMPS, 8, LANES), np.float32)
    for row, column in enumerate([centre, np.abs(u), np.abs(v)]):
        scalars[:, row, :LOCAL] = column.reshape(COMPS, LOCAL)
    return table.reshape(COMPS, LOCAL, LANES), scalars


def energy_scale():
    return float(1.0 / (NDIR * np.sum(1.1 ** (np.arange(NFREQ) - NFREQ // 2.0))))


def shifted(me, step):
    z = (me // 8 + step // 8) % 8
    y = ((me // 2) % 4 + (step // 2) % 4) % 4
    core = (me % 2 + step % 2) % 2
    return z * 8 + y * 2 + core


def gathered(source, lanes):
    return jnp.take_along_axis(source, lanes, axis=1, mode="promise_in_bounds")


def spread_rows(row):
    return jnp.broadcast_to(row, (LOCAL, LANES))


def exchange_kernel(
    spectrum, wind_field, sea_table, transfer, table, scalars,
    result,
    wave0, wave1, mask, sea_rows, lane_map, part_map, units, units_smem, scalars_smem,
    wind, kernel_buf, constants, own, omega, cosine, sine,
    to_west, to_east, from_west, from_east,
    outgoing, incoming, dense, rounded, coupled, returning, arrived_a, arrived_b, expanded, spread,
    load_sem, comp_sem, halo_send, halo_recv, send_sem, forward_sem, back_sem, store_sem,
):
    me = lax.axis_index("comp")
    region = lax.axis_index("region")
    west = (region + REGIONS - 1) % REGIONS
    east = (region + 1) % REGIONS

    def comp_load(comp):
        return pltpu.make_async_copy(
            spectrum.at[comp], wave0.at[pl.ds(pl.multiple_of(comp * STRIDE + 8, 8), ROWS)], comp_sem.at[comp])

    load_scalars = pltpu.make_async_copy(scalars.at[me], scalars_smem, load_sem.at[0])
    load_scalars.start()
    load_own = pltpu.make_async_copy(table.at[me], own, load_sem.at[1])
    load_own.start()

    @pl.loop(0, LOCAL)
    def _(comp):
        comp_load(comp).start()

    barrier = pltpu.get_barrier_semaphore()

    @pl.loop(1, COMPS)
    def _(step):
        pl.semaphore_signal(barrier, inc=1, device_id={"comp": shifted(me, step)}, device_id_type=MESH)

    pl.semaphore_signal(barrier, inc=1, device_id={"region": west}, device_id_type=MESH)
    pl.semaphore_signal(barrier, inc=1, device_id={"region": east}, device_id_type=MESH)

    load_constants = pltpu.make_async_copy(table, constants, load_sem.at[2])
    load_constants.start()
    load_kernel = pltpu.make_async_copy(transfer, kernel_buf, load_sem.at[3])
    load_kernel.start()
    load_wind = pltpu.make_async_copy(wind_field, wind.at[pl.ds(0, 2 * ROWS)], load_sem.at[4])
    load_wind.start()

    for part in range(4):
        sea_rows[pl.ds(part, BLOCKS, stride=4), :] = sea_table[:, part * LANES : (part + 1) * LANES]

    row_number = lax.broadcasted_iota(jnp.int32, (ROWS, LANES), 0)
    lane_position = lax.broadcasted_iota(jnp.int32, (ROWS, LANES), 1)
    later = (sea_rows[0:ROWS, :] >= 0) & ((row_number & 3) > 0)
    count = jnp.where(later, 1.0, 0.0)
    lower = jnp.where(
        lax.broadcasted_iota(jnp.int32, (ROWS, ROWS), 0) > lax.broadcasted_iota(jnp.int32, (ROWS, ROWS), 1), 1.0, 0.0
    ).astype(jnp.bfloat16)
    rank = jnp.dot(lower, count.astype(jnp.bfloat16), preferred_element_type=F32)
    found = jnp.where((rank == lane_position.astype(F32)) & later, row_number.astype(F32), 0.0)
    before = jnp.where(row_number < lane_position * 4, count, 0.0)
    unit_rows = jnp.broadcast_to(jnp.sum(found, axis=0, keepdims=True), (4, LANES))
    first_units = jnp.broadcast_to(jnp.sum(before, axis=0, keepdims=True), (4, LANES))
    units[...] = jnp.concatenate([unit_rows, first_units], axis=0).astype(jnp.int32)
    load_units = pltpu.make_async_copy(units, units_smem, load_sem.at[5])
    load_units.start()

    lane_number = lax.broadcasted_iota(jnp.int32, (LANES, 4 * LANES), 0)
    quarter = lax.broadcasted_iota(jnp.int32, (8, 4 * LANES), 0)

    def listed_maps(block, weights):
        cells = sea_table[pl.ds(block, 1), :]
        lane = jnp.where(cells >= 0, cells & (LANES - 1), -1)
        inside = jnp.where(cells >= 0, (cells >> 7) & 3, -1)
        match = jnp.where(lane == lane_number, 1.0, 0.0).astype(jnp.bfloat16)
        row = jnp.where(inside == quarter, 1.0, 0.0)
        rows = jnp.concatenate([row * w for w in weights], axis=0).astype(jnp.bfloat16)
        return lax.dot_general(rows, match, (((1,), (1,)), ((), ())), preferred_element_type=F32)

    def block_rows(block):
        return pl.ds(pl.multiple_of(block * 4, 4), 4)

    @pl.loop(0, BLOCKS, unroll=8)
    def _(block):
        mask[block_rows(block), :] = listed_maps(block, [1.0])[0:4]

    def strided(x):
        return pl.ds(x, LOCAL, stride=STRIDE)

    @pl.loop(0, LOCAL)
    def _(comp):
        comp_load(comp).wait()
        base = pl.multiple_of(comp * STRIDE + 8, 8)
        for start in range(0, ROWS, 64):
            rows = pl.ds(base + start, 64)
            wave0[rows, :] = mask[start : start + 64, :] * wave0[rows, :]

    first_row, last_row = wave0[strided(8), :], wave0[strided(7 + ROWS), :]
    to_west[0] = first_row
    to_west[1] = wave0[strided(9), :]
    to_west[2] = spread_rows(mask[0:1, :])
    to_east[0] = last_row
    to_east[1] = wave0[strided(6 + ROWS), :]
    to_east[2] = spread_rows(mask[ROWS - 1 : ROWS, :])
    pl.semaphore_wait(barrier, COMPS + 1)
    send_west = pltpu.make_async_remote_copy(
        to_west, from_east, halo_send.at[0], halo_recv.at[0], device_id={"region": west}, device_id_type=MESH)
    send_east = pltpu.make_async_remote_copy(
        to_east, from_west, halo_send.at[1], halo_recv.at[1], device_id={"region": east}, device_id_type=MESH)
    send_west.start()
    send_east.start()

    load_scalars.wait()
    lanes = lax.broadcasted_iota(jnp.int32, (8, LANES), 1)

    def substep(source, target, groups):
        @pl.loop(0, LOCAL)
        def _(comp):
            direction = (me * LOCAL + comp) % NDIR
            aside = jnp.where((direction < NDIR // 4) | (direction >= 3 * NDIR // 4), -1, 1)
            turn = jnp.where(direction < NDIR // 2, 1, LANES - 1)
            edge = jnp.where(direction < NDIR // 2, 0, LANES - 1)
            centre_w = jnp.full((8, LANES), scalars_smem[0, comp])
            x_w = jnp.full((8, LANES), scalars_smem[1, comp])
            y_w = jnp.where(lanes == edge, 0.0, scalars_smem[2, comp])
            base = pl.multiple_of(comp * STRIDE + 8, 8)
            for group in groups:
                here = source[pl.ds(base + 8 * group, 8), :]
                beside = source[pl.ds(base + 8 * group + aside, 8), :]
                changed = centre_w * here + x_w * beside + y_w * pltpu.roll(here, turn, 1)
                target[pl.ds(base + 8 * group, 8), :] = mask[8 * group : 8 * group + 8, :] * changed

    substep(wave0, wave1, range(1, ROWS // 8 - 1))

    load_own.wait()
    coefficients = own[...]
    wide = lax.broadcasted_iota(jnp.int32, (LOCAL, LANES), 1)

    def column(number):
        return spread_rows(coefficients[:, number : number + 1])

    centre_w, west_w, east_w = column(3), column(4), column(5)
    south_w = jnp.where(wide == 0, 0.0, column(6))
    north_w = jnp.where(wide == LANES - 1, 0.0, column(7))

    def halo(rows, inside, outermost, before):
        near = jnp.where(inside, rows[0], 0.0)
        far = jnp.where(inside, rows[1], 0.0)
        sides = (far, outermost) if before else (outermost, far)
        changed = (
            centre_w * near + west_w * sides[0] + east_w * sides[1]
            + south_w * pltpu.roll(near, 1, 1) + north_w * pltpu.roll(near, LANES - 1, 1)
        )
        at = strided(7 if before else 8 + ROWS)
        wave0[at, :] = near
        wave1[at, :] = rows[2] * changed

    send_west.wait()
    send_east.wait()
    halo(from_west, region > 0, first_row, True)
    halo(from_east, region < REGIONS - 1, last_row, False)
    substep(wave0, wave1, (0, ROWS // 8 - 1))
    substep(wave1, wave0, range(ROWS // 8))

    load_units.wait()

    def packed(row):
        cells = sea_rows[pl.ds(row, 1), :]
        base = row & ~3
        lane = spread_rows(cells & (LANES - 1))
        inside = spread_rows((cells >> 7) & 3)
        total = gathered(wave0[strided(8 + base), :], lane)
        for number in range(1, 4):
            total = jnp.where(inside == number, gathered(wave0[strided(8 + base + number), :], lane), total)
        return total

    def unit_row(chunk, device):
        return jnp.clip(units_smem[0, device], 0, ROWS - 1) if chunk == 0 else device * 4

    def forward(chunk, target):
        return pltpu.make_async_remote_copy(
            outgoing.at[chunk, target], incoming.at[chunk, me], send_sem.at[chunk], forward_sem.at[chunk, me],
            device_id={"comp": target}, device_id_type=MESH)

    for chunk in range(2):

        @pl.loop(1, COMPS)
        def _(step, chunk=chunk):
            target = shifted(me, step)
            outgoing[chunk, target] = packed(unit_row(chunk, target))
            forward(chunk, target).start()

    for chunk in range(2):
        incoming[chunk, me] = packed(unit_row(chunk, me))

    load_constants.wait()

    @pl.loop(0, COMPS, unroll=4)
    def _(source):
        values = constants[source]
        omega[source] = spread_rows(values[:, 0:1])
        cosine[source] = spread_rows(values[:, 1:2])
        sine[source] = spread_rows(values[:, 2:3])

    slot = lax.broadcasted_iota(jnp.int32, (1, 4 * LANES), 1)
    slot_lane = (slot & (LANES - 1)).astype(F32)
    slot_part = (slot >> 7).astype(F32)

    @pl.loop(0, BLOCKS, unroll=8)
    def _(block):
        maps = listed_maps(block, [slot_lane, slot_part])
        rows = block_rows(block)
        lane_map[rows, :] = maps[0:4].astype(jnp.int32)
        part_map[rows, :] = jnp.where(mask[rows, :] > 0.5, maps[8:12], -1.0).astype(jnp.int32)

    load_kernel.wait()
    load_wind.wait()

    def wind_at(row):
        cells = sea_rows[pl.ds(row, 1), :]
        base = row & ~3
        lane = jnp.broadcast_to(cells & (LANES - 1), (8, LANES))
        inside = (cells >> 7) & 3
        parts = []
        for part in range(2):
            total = jnp.zeros((8, LANES), F32)
            for number in range(4):
                line = jnp.broadcast_to(wind[pl.ds(part * ROWS + base + number, 1), :], (8, LANES))
                total = jnp.where(inside == number, gathered(line, lane), total)
            parts.append(total[0:1])
        return parts

    def back(chunk, target, held):
        return pltpu.make_async_remote_copy(
            returning.at[chunk, target], held.at[me], send_sem.at[2 + chunk], back_sem.at[chunk, me],
            device_id={"comp": target}, device_id_type=MESH)

    for chunk, held in enumerate((arrived_a, arrived_b)):

        @pl.loop(1, COMPS)
        def _(step, chunk=chunk):
            source = shifted(me, step)
            pltpu.make_async_remote_copy(
                outgoing.at[chunk, source], incoming.at[chunk, source], send_sem.at[chunk], forward_sem.at[chunk, source],
                device_id={"comp": source}, device_id_type=MESH).wait_recv()

        wind_u, wind_v = wind_at(unit_row(chunk, me))

        def collect(source, total, chunk=chunk):
            values = incoming[chunk, source]
            dense[pl.ds(source * LOCAL, LOCAL), :] = values
            return total + omega[source] * values

        total = lax.fori_loop(0, COMPS, collect, jnp.zeros((LOCAL, LANES), F32), unroll=True)
        energy = jnp.sum(total, axis=0, keepdims=True) * energy_scale()
        loss = dissipation * energy * energy
        rounded[...] = dense[0:SPEC, :].astype(jnp.bfloat16)

        @pl.loop(0, SPEC // TILE)
        def _(tile):
            rows = pl.ds(pl.multiple_of(tile * TILE, TILE), TILE)
            coupled[rows, :] = jnp.dot(kernel_buf[rows, :], rounded[...], preferred_element_type=F32)

        def updated(target, chunk=chunk, wind_u=wind_u, wind_v=wind_v, loss=loss):
            points = incoming[chunk, target]
            speed = omega[target]
            along = cosine[target] * wind_u + sine[target] * wind_v
            growth = growth_rate * speed * jnp.maximum(along - wind_floor, 0.0)
            damping = speed * speed * loss
            joined = coupled[pl.ds(target * LOCAL, LOCAL), :]
            return points + points * (growth - damping + coupling * joined) / (1.0 + damping)

        @pl.loop(1, COMPS)
        def _(step, chunk=chunk, held=held, updated=updated):
            target = shifted(me, step)
            returning[chunk, target] = updated(target)
            back(chunk, target, held).start()

        held[me] = updated(me)

    def wait_back(chunk, source, held):
        pltpu.make_async_remote_copy(
            returning.at[chunk, source], held.at[source], send_sem.at[2 + chunk], back_sem.at[chunk, source],
            device_id={"comp": source}, device_id_type=MESH).wait_recv()

    @pl.loop(1, COMPS)
    def _(step):
        wait_back(0, shifted(me, step), arrived_a)

    @pl.loop(0, BLOCKS)
    def _(block):
        first_unit = units_smem[4, block]
        pieces = []
        for number in range(4):
            line = pl.ds(block * 4 + number, 1)
            lane, part = spread_rows(lane_map[line, :]), spread_rows(part_map[line, :])
            total = jnp.zeros((LOCAL, LANES), F32)
            for offset in range(3):
                values = arrived_a[jnp.clip(first_unit + offset, 0, COMPS - 1)]
                total = jnp.where(part == offset + 1, gathered(values, lane), total)
            pieces.append(total)
        for number in range(4):
            expanded[block * 4 + number] = pieces[number]

    def store(chip):
        return pltpu.make_async_copy(
            spread.at[chip, pl.ds(0, LOCAL * 8)].reshape(LOCAL, 8, LANES),
            result.at[:, pl.ds(pl.multiple_of(chip * 8, 8), 8), :], store_sem.at[0])

    def finish(chip):
        pieces = []
        for core in range(2):
            values = arrived_b[2 * chip + core]
            for number in range(4):
                x = chip * 8 + core * 4 + number
                line = pl.ds(x, 1)
                lane, part = spread_rows(lane_map[line, :]), spread_rows(part_map[line, :])
                pieces.append(jnp.where(part == 0, gathered(values, lane), expanded[x]))
        for number, piece in enumerate(pieces):
            spread[chip, pl.ds(number, LOCAL, stride=8), :] = piece
        store(chip).start()

    wait_back(1, shifted(me, 1), arrived_b)
    finish(me // 2)

    @pl.loop(1, COMPS // 2)
    def _(step):
        chip = (me // 8 + 8 - step // 4) % 8 * 4 + ((me // 2) % 4 + 4 - step % 4) % 4
        wait_back(1, 2 * chip, arrived_b)
        wait_back(1, 2 * chip + 1, arrived_b)
        finish(chip)

    for number in range(4):
        sent = outgoing.at[0, pl.ds(0, COMPS - 1)]
        pltpu.make_async_copy(sent, sent, send_sem.at[number]).wait()
    pltpu.make_async_copy(result, result, store_sem.at[0]).wait()


def on_device(spectrum, wind, sea_table, transfer_kernel):
    table, scalars = (jnp.asarray(array) for array in component_tables())
    vmem = pl.BlockSpec(memory_space=pltpu.VMEM)
    anywhere = pl.BlockSpec(memory_space=pl.ANY)
    wave = pltpu.VMEM((PADDED_COMP * STRIDE, LANES), F32)
    line_map = pltpu.VMEM((PADDED_ROWS, LANES), jnp.int32)
    per_source = pltpu.VMEM((COMPS, LOCAL, LANES), F32)
    per_chunk = pltpu.VMEM((2, COMPS, LOCAL, LANES), F32)
    rim = pltpu.VMEM((3, LOCAL, LANES), F32)
    dense = pltpu.VMEM((PADDED_SPEC, LANES), F32)
    dma = pltpu.SemaphoreType.DMA
    return pl.pallas_call(
        exchange_kernel,
        out_shape=jax.ShapeDtypeStruct((LOCAL, ROWS, LANES), F32),
        in_specs=[anywhere, anywhere, vmem, anywhere, anywhere, anywhere],
        out_specs=anywhere,
        scratch_shapes=[
            wave,
            wave,
            pltpu.VMEM((PADDED_ROWS, LANES), F32),
            line_map,
            line_map,
            line_map,
            pltpu.VMEM((8, LANES), jnp.int32),
            pltpu.SMEM((8, LANES), jnp.int32),
            pltpu.SMEM((8, LANES), F32),
            pltpu.VMEM((2 * ROWS + 8, LANES), F32),
            pltpu.VMEM((SPEC, SPEC), jnp.bfloat16),
            per_source,
            pltpu.VMEM((LOCAL, LANES), F32),
            per_source,
            per_source,
            per_source,
            rim,
            rim,
            rim,
            rim,
            per_chunk,
            per_chunk,
            dense,
            pltpu.VMEM((SPEC, LANES), jnp.bfloat16),
            dense,
            per_chunk,
            per_source,
            per_source,
            pltpu.VMEM((ROWS, LOCAL, LANES), F32),
            pltpu.VMEM((COMPS // 2, 256, LANES), F32),
            dma((6,)),
            dma((LOCAL,)),
            dma((2,)),
            dma((2,)),
            dma((4,)),
            dma((2, COMPS)),
            dma((2, COMPS)),
            dma((1,)),
        ],
        compiler_params=pltpu.CompilerParams(
            collective_id=0, has_side_effects=True, vmem_limit_bytes=56 * 1024 * 1024
        ),
        cost_estimate=pl.CostEstimate(flops=2 * SPEC * SPEC * 256, bytes_accessed=16 << 20, transcendentals=0),
        name="exchange",
    )(spectrum, wind.reshape(2 * ROWS, LANES), sea_table, transfer_kernel, table, scalars)


def solution(mesh):
    placed = (P("comp", "region", None), P(None, "region", None), P("region", None), P())
    return jax.shard_map(
        on_device, mesh=mesh, in_specs=placed, out_specs=P("comp", "region", None), check_vma=False
    )
```

```python
import math

import jax
import jax.numpy as jnp
import numpy as np
from jax import lax
from jax.experimental import pallas as pl
from jax.experimental.pallas import tpu as pltpu
from jax.sharding import PartitionSpec as P

NDIR = 36
NFREQ = 48
SPEC = NDIR * NFREQ
COMPS = 64
LOCAL = SPEC // COMPS
REGIONS = 4
ROWS = 256
LANES = 128
BLOCKS = 64
STRIDE = ROWS + 16
PADDED_ROWS = ROWS + 8
PADDED_COMP = 32
PADDED_SPEC = SPEC + 32
TILE = 432
EARLY = 20
SHARE = 9
F32 = jnp.float32
MESH = pl.DeviceIdType.MESH

growth_rate = 0.05
wind_floor = 0.5
dissipation = 0.02
coupling = 0.5
courant_top = 0.6


def component_tables():
    comp = np.arange(SPEC)
    freq, direction = comp // NDIR, 2.0 * math.pi * (comp % NDIR + 0.5) / NDIR
    omega = 1.1 ** (freq - NFREQ // 2)
    speed = courant_top * 1.1 ** (-freq.astype(np.float64))
    cosine, sine = np.cos(direction), np.sin(direction)
    u, v = speed * cosine, speed * sine
    centre = 1.0 - np.abs(u) - np.abs(v)
    columns = [omega, cosine, sine, centre, np.maximum(u, 0), np.maximum(-u, 0), np.maximum(v, 0), np.maximum(-v, 0)]
    table = np.zeros((SPEC, LANES), np.float32)
    for lane, column in enumerate(columns):
        table[:, lane] = column
    scalars = np.zeros((COMPS, 8, LANES), np.float32)
    for row, column in enumerate([centre, np.abs(u), np.abs(v)]):
        scalars[:, row, :LOCAL] = column.reshape(COMPS, LOCAL)
    return table.reshape(COMPS, LOCAL, LANES), scalars


def energy_scale():
    return float(1.0 / (NDIR * np.sum(1.1 ** (np.arange(NFREQ) - NFREQ // 2.0))))


def shifted(me, step):
    z = ((me & 56) + (step & 56)) & 56
    y = ((me & 6) + (step & 6)) & 6
    return z + y + ((me + step) & 1)


def gathered(source, lanes):
    return jnp.take_along_axis(source, lanes, axis=1, mode="promise_in_bounds")


def spread_rows(row):
    return jnp.broadcast_to(row, (LOCAL, LANES))


def exchange_kernel(
    spectrum, wind_field, listed, transfer, table, scalars,
    result,
    wave0, wave1, wave2, sea_table, mask, sea_rows, lane_map, part_map, units, units_smem, scalars_smem,
    wind, kernel_buf, constants, own, omega, cosine, sine,
    to_west, to_east, from_west, from_east,
    outgoing, incoming, dense, rounded, coupled, returning, arrived_a, arrived_b, expanded,
    load_sem, comp_sem, halo_send, halo_recv, send_sem, forward_sem, back_sem,
):
    me = lax.axis_index("comp")
    region = lax.axis_index("region")
    west = (region + REGIONS - 1) & (REGIONS - 1)
    east = (region + 1) & (REGIONS - 1)

    def comp_load(comp):
        return pltpu.make_async_copy(
            spectrum.at[comp], wave0.at[pl.ds(comp * STRIDE + 8, ROWS)], comp_sem.at[comp // SHARE])

    barrier = pltpu.get_barrier_semaphore()

    for step in range(1, COMPS):
        pl.semaphore_signal(barrier, inc=1, device_id={"comp": shifted(me, step)}, device_id_type=MESH)
    pl.semaphore_signal(barrier, inc=1, device_id={"region": west}, device_id_type=MESH)
    pl.semaphore_signal(barrier, inc=1, device_id={"region": east}, device_id_type=MESH)

    load_listed = pltpu.make_async_copy(listed, sea_table, load_sem.at[6])
    load_listed.start()

    for comp in range(LOCAL):
        comp_load(comp).start()

    load_scalars = pltpu.make_async_copy(scalars.at[me], scalars_smem, load_sem.at[0])
    load_scalars.start()
    load_own = pltpu.make_async_copy(table.at[me], own, load_sem.at[1])
    load_own.start()
    load_constants = pltpu.make_async_copy(table, constants, load_sem.at[2])
    load_kernel = pltpu.make_async_copy(transfer, kernel_buf, load_sem.at[3])
    load_wind = pltpu.make_async_copy(wind_field, wind.at[pl.ds(0, 2 * ROWS)], load_sem.at[4])
    load_listed.wait()

    for part in range(4):
        sea_rows[pl.ds(part, BLOCKS, stride=4), :] = sea_table[:, part * LANES : (part + 1) * LANES]

    lane_number = lax.broadcasted_iota(jnp.int32, (LANES, 4 * LANES), 0)
    quarter = lax.broadcasted_iota(jnp.int32, (8, 4 * LANES), 0)

    def listed_maps(block, weights):
        cells = sea_table[pl.ds(block, 1), :]
        lane = jnp.where(cells >= 0, cells & (LANES - 1), -1)
        inside = jnp.where(cells >= 0, (cells >> 7) & 3, -1)
        match = jnp.where(lane == lane_number, 1.0, 0.0).astype(jnp.bfloat16)
        row = jnp.where(inside == quarter, 1.0, 0.0)
        rows = jnp.concatenate([row * w for w in weights], axis=0).astype(jnp.bfloat16)
        return lax.dot_general(rows, match, (((1,), (1,)), ((), ())), preferred_element_type=F32)

    def block_rows(block):
        return pl.ds(pl.multiple_of(block * 4, 4), 4)

    @pl.loop(0, BLOCKS, unroll=8)
    def _(block):
        mask[block_rows(block), :] = listed_maps(block, [1.0])[0:4]

    def strided(x):
        return pl.ds(x, LOCAL, stride=STRIDE)

    for share in range(LOCAL // SHARE):
        landed = wave0.at[pl.ds(0, SHARE * ROWS)]
        pltpu.make_async_copy(landed, landed, comp_sem.at[share]).wait()

        @pl.loop(share * SHARE, (share + 1) * SHARE)
        def _(comp):
            base = pl.multiple_of(comp * STRIDE + 8, 8)
            for start in range(0, ROWS, 64):
                rows = pl.ds(base + start, 64)
                wave0[rows, :] = mask[start : start + 64, :] * wave0[rows, :]

    nothing = jnp.zeros((LOCAL, LANES), F32)
    for wave in (wave0, wave1):
        wave[strided(7), :] = nothing
        wave[strided(8 + ROWS), :] = nothing

    first_row, last_row = wave0[strided(8), :], wave0[strided(7 + ROWS), :]
    to_west[0] = first_row
    to_west[1] = wave0[strided(9), :]
    to_west[2] = spread_rows(mask[0:1, :])
    to_east[0] = last_row
    to_east[1] = wave0[strided(6 + ROWS), :]
    to_east[2] = spread_rows(mask[ROWS - 1 : ROWS, :])
    pl.semaphore_wait(barrier, COMPS + 1)
    send_west = pltpu.make_async_remote_copy(
        to_west, from_east, halo_send.at[0], halo_recv.at[0], device_id={"region": west}, device_id_type=MESH)
    send_east = pltpu.make_async_remote_copy(
        to_east, from_west, halo_send.at[1], halo_recv.at[1], device_id={"region": east}, device_id_type=MESH)
    send_west.start()
    send_east.start()

    load_scalars.wait()
    lanes = lax.broadcasted_iota(jnp.int32, (8, LANES), 1)

    def substep(source, target, groups, unroll, origin=0):
        @pl.loop(0, LOCAL, unroll=unroll)
        def _(comp):
            direction = lax.rem(me * LOCAL + comp, NDIR)
            aside = jnp.where((direction < NDIR // 4) | (direction >= 3 * NDIR // 4), -1, 1)
            turn = jnp.where(direction < NDIR // 2, 1, LANES - 1)
            edge = jnp.where(direction < NDIR // 2, 0, LANES - 1)
            centre_w = jnp.full((8, LANES), scalars_smem[0, comp])
            x_w = jnp.full((8, LANES), scalars_smem[1, comp])
            y_w = jnp.where(lanes == edge, 0.0, scalars_smem[2, comp])
            for group in groups:
                row = pl.multiple_of(origin + 8 * group, 8)
                base = pl.multiple_of(comp * STRIDE + 8 + row, 8)
                here = source[pl.ds(base, 8), :]
                beside = source[pl.ds(base + aside, 8), :]
                changed = centre_w * here + x_w * beside + y_w * pltpu.roll(here, turn, 1)
                target[pl.ds(base, 8), :] = mask[pl.ds(row, 8), :] * changed

    substep(wave0, wave1, range(ROWS // 8), 3)

    def packed(row):
        cells = sea_rows[pl.ds(row, 1), :]
        base = row & ~3
        lane = spread_rows(cells & (LANES - 1))
        inside = spread_rows((cells >> 7) & 3)
        total = gathered(wave2[strided(8 + base), :], lane)
        for number in range(1, 4):
            total = jnp.where(inside == number, gathered(wave2[strided(8 + base + number), :], lane), total)
        return total

    def unit_row(chunk, device):
        return jnp.clip(units_smem[0, device], 0, ROWS - 1) if chunk == 0 else device * 4

    def forward(chunk, target):
        return pltpu.make_async_remote_copy(
            outgoing.at[chunk, target], incoming.at[chunk, me], send_sem.at[chunk], forward_sem.at[chunk],
            device_id={"comp": target}, device_id_type=MESH)

    def send(chunk, target):
        outgoing[chunk, target] = packed(unit_row(chunk, target))
        forward(chunk, target).start()

    def quarter_sends(number, order):
        part = ((me >> 4) + order) & 3
        substep(wave1, wave2, range(8), 9, origin=part * 64)

        @pl.loop(0, 16)
        def _(place):
            target = part * 16 + ((me + place) & 15)
            ready = (target >= 4) & (target < BLOCKS - 4) if number == 0 else target != me

            @pl.when(ready)
            def _():
                send(1, target)

    quarter_sends(0, 2)
    load_kernel.start()
    load_constants.start()
    load_wind.start()

    load_own.wait()
    coefficients = own[...]
    wide = lax.broadcasted_iota(jnp.int32, (LOCAL, LANES), 1)

    def column(number):
        return spread_rows(coefficients[:, number : number + 1])

    centre_w, west_w, east_w = column(3), column(4), column(5)
    south_w = jnp.where(wide == 0, 0.0, column(6))
    north_w = jnp.where(wide == LANES - 1, 0.0, column(7))

    def halo(rows, inside, outermost, before):
        near = jnp.where(inside, rows[0], 0.0)
        far = jnp.where(inside, rows[1], 0.0)
        sides = (far, outermost) if before else (outermost, far)
        changed = (
            centre_w * near + west_w * sides[0] + east_w * sides[1]
            + south_w * pltpu.roll(near, 1, 1) + north_w * pltpu.roll(near, LANES - 1, 1)
        )
        at = strided(7 if before else 8 + ROWS)
        wave0[at, :] = near
        wave1[at, :] = rows[2] * changed

    send_west.wait()
    send_east.wait()
    halo(from_west, region > 0, first_row, True)
    halo(from_east, region < REGIONS - 1, last_row, False)
    substep(wave0, wave1, (0, ROWS // 8 - 1), 9)
    substep(wave1, wave2, (0, ROWS // 8 - 1), 9)
    quarter_sends(1, 1)

    row_number = lax.broadcasted_iota(jnp.int32, (ROWS, LANES), 0)
    lane_position = lax.broadcasted_iota(jnp.int32, (ROWS, LANES), 1)
    later = (sea_rows[0:ROWS, :] >= 0) & ((row_number & 3) > 0)
    count = jnp.where(later, 1.0, 0.0)
    lower = jnp.where(
        lax.broadcasted_iota(jnp.int32, (ROWS, ROWS), 0) > lax.broadcasted_iota(jnp.int32, (ROWS, ROWS), 1), 1.0, 0.0
    ).astype(jnp.bfloat16)
    rank = jnp.dot(lower, count.astype(jnp.bfloat16), preferred_element_type=F32)
    found = jnp.where((rank == lane_position.astype(F32)) & later, row_number.astype(F32), 0.0)
    before = jnp.where(row_number < lane_position * 4, count, 0.0)
    unit_rows = jnp.broadcast_to(jnp.sum(found, axis=0, keepdims=True), (4, LANES))
    first_units = jnp.broadcast_to(jnp.sum(before, axis=0, keepdims=True), (4, LANES))
    units[...] = jnp.concatenate([unit_rows, first_units], axis=0).astype(jnp.int32)
    load_units = pltpu.make_async_copy(units, units_smem, load_sem.at[5])
    load_units.start()

    quarter_sends(2, 3)
    quarter_sends(3, 0)

    @pl.loop(0, 4)
    def _(place):
        part = ((me >> 4) + 2) & 3

        @pl.when((part == 0) | (part == 3))
        def _():
            send(1, part * 20 + ((me + place) & 3))

    load_units.wait()

    @pl.loop(1, COMPS)
    def _(step):
        send(0, shifted(me, step))

    for chunk in range(2):
        incoming[chunk, me] = packed(unit_row(chunk, me))

    load_constants.wait()

    @pl.loop(0, COMPS, unroll=4)
    def _(source):
        values = constants[source]
        omega[source] = spread_rows(values[:, 0:1])
        cosine[source] = spread_rows(values[:, 1:2])
        sine[source] = spread_rows(values[:, 2:3])

    slot = lax.broadcasted_iota(jnp.int32, (1, 4 * LANES), 1)
    slot_lane = (slot & (LANES - 1)).astype(F32)
    slot_part = (slot >> 7).astype(F32)

    @pl.loop(0, BLOCKS, unroll=8)
    def _(block):
        maps = listed_maps(block, [slot_lane, slot_part])
        rows = block_rows(block)
        lane_map[rows, :] = maps[0:4].astype(jnp.int32)
        part_map[rows, :] = jnp.where(mask[rows, :] > 0.5, maps[8:12], -1.0).astype(jnp.int32)

    load_kernel.wait()
    load_wind.wait()

    def wind_at(row):
        cells = sea_rows[pl.ds(row, 1), :]
        base = row & ~3
        lane = jnp.broadcast_to(cells & (LANES - 1), (8, LANES))
        inside = (cells >> 7) & 3
        parts = []
        for part in range(2):
            total = jnp.zeros((8, LANES), F32)
            for number in range(4):
                line = jnp.broadcast_to(wind[pl.ds(part * ROWS + base + number, 1), :], (8, LANES))
                total = jnp.where(inside == number, gathered(line, lane), total)
            parts.append(total[0:1])
        return parts

    def back(chunk, target, held):
        return pltpu.make_async_remote_copy(
            returning.at[chunk, target], held.at[me], send_sem.at[2 + chunk], back_sem.at[(1 + (me >> 3)) * chunk],
            device_id={"comp": target}, device_id_type=MESH)

    def source_terms(chunk, held):
        landed = incoming.at[chunk, pl.ds(0, COMPS - 1)]
        pltpu.make_async_copy(landed, landed, forward_sem.at[chunk]).wait()
        wind_u, wind_v = wind_at(unit_row(chunk, me))

        def collect(source, total):
            values = incoming[chunk, source]
            dense[pl.ds(source * LOCAL, LOCAL), :] = values
            return total + omega[source] * values

        total = lax.fori_loop(0, COMPS, collect, jnp.zeros((LOCAL, LANES), F32), unroll=True)
        energy = jnp.sum(total, axis=0, keepdims=True) * energy_scale()
        loss = dissipation * energy * energy
        rounded[...] = dense[0:SPEC, :].astype(jnp.bfloat16)

        @pl.loop(0, SPEC // TILE)
        def _(tile):
            rows = pl.ds(pl.multiple_of(tile * TILE, TILE), TILE)
            coupled[rows, :] = jnp.dot(kernel_buf[rows, :], rounded[...], preferred_element_type=F32)

        def updated(target):
            points = incoming[chunk, target]
            speed = omega[target]
            along = cosine[target] * wind_u + sine[target] * wind_v
            growth = growth_rate * speed * jnp.maximum(along - wind_floor, 0.0)
            damping = speed * speed * loss
            joined = coupled[pl.ds(target * LOCAL, LOCAL), :]
            return points + points * (growth - damping + coupling * joined) / (1.0 + damping)

        held[me] = updated(me)
        return updated

    updated = source_terms(1, arrived_b)

    @pl.loop(1, EARLY)
    def _(step):
        target = shifted(me, step)
        returning[1, target] = updated(target)
        back(1, target, arrived_b).start()

    @pl.loop(EARLY, COMPS)
    def _(step):
        target = shifted(me, step)
        returning[1, target] = updated(target)

    updated_later = source_terms(0, arrived_a)

    @pl.loop(1, COMPS)
    def _(step):
        target = shifted(me, step)
        returning[0, target] = updated_later(target)
        back(0, target, arrived_a).start()

    @pl.loop(EARLY, COMPS)
    def _(step):
        back(1, shifted(me, step), arrived_b).start()

    landed = arrived_a.at[pl.ds(0, COMPS - 1)]
    pltpu.make_async_copy(landed, landed, back_sem.at[0]).wait()

    @pl.loop(0, BLOCKS)
    def _(block):
        first_unit = units_smem[4, block]
        pieces = []
        for number in range(4):
            line = pl.ds(block * 4 + number, 1)
            lane, part = spread_rows(lane_map[line, :]), spread_rows(part_map[line, :])
            total = jnp.zeros((LOCAL, LANES), F32)
            for offset in range(3):
                values = arrived_a[jnp.clip(first_unit + offset, 0, COMPS - 1)]
                total = jnp.where(part == offset + 1, gathered(values, lane), total)
            pieces.append(total)
        for number in range(4):
            expanded[block * 4 + number] = pieces[number]

    def finish(block):
        values = arrived_b[block]
        for number in range(4):
            x = block * 4 + number
            line = pl.ds(x, 1)
            lane, part = spread_rows(lane_map[line, :]), spread_rows(part_map[line, :])
            piece = jnp.where(part == 0, gathered(values, lane), expanded[x])
            result[pl.ds(x, LOCAL, stride=ROWS), :] = piece

    for step in range(8):
        plane = ((me >> 3) + 8 - step) & 7
        landed = arrived_b.at[pl.ds(0, 8 if step else 7)]
        pltpu.make_async_copy(landed, landed, back_sem.at[1 + plane]).wait()

        @pl.loop(0, 8, unroll=4)
        def _(place, plane=plane):
            finish(plane * 8 + place)

    for number in range(4):
        sent = outgoing.at[0, pl.ds(0, COMPS - 1)]
        pltpu.make_async_copy(sent, sent, send_sem.at[number]).wait()


def on_device(spectrum, wind, sea_table, transfer_kernel):
    table, scalars = (jnp.asarray(array) for array in component_tables())
    anywhere = pl.BlockSpec(memory_space=pltpu.HBM)
    wave = pltpu.VMEM((PADDED_COMP * STRIDE, LANES), F32)
    line_map = pltpu.VMEM((PADDED_ROWS, LANES), jnp.int32)
    per_source = pltpu.VMEM((COMPS, LOCAL, LANES), F32)
    per_chunk = pltpu.VMEM((2, COMPS, LOCAL, LANES), F32)
    rim = pltpu.VMEM((3, LOCAL, LANES), F32)
    dense = pltpu.VMEM((PADDED_SPEC, LANES), F32)
    dma = pltpu.SemaphoreType.DMA
    result = pl.pallas_call(
        exchange_kernel,
        out_shape=pltpu.VMEM((PADDED_COMP * ROWS, LANES), F32),
        in_specs=[anywhere] * 6,
        out_specs=pl.BlockSpec(memory_space=pltpu.VMEM),
        scratch_shapes=[
            wave,
            wave,
            wave,
            pltpu.VMEM((BLOCKS, 4 * LANES), jnp.int32),
            pltpu.VMEM((PADDED_ROWS, LANES), F32),
            line_map,
            line_map,
            line_map,
            pltpu.VMEM((8, LANES), jnp.int32),
            pltpu.SMEM((8, LANES), jnp.int32),
            pltpu.SMEM((8, LANES), F32),
            pltpu.VMEM((2 * ROWS + 8, LANES), F32),
            pltpu.VMEM((SPEC, SPEC), jnp.bfloat16),
            per_source,
            pltpu.VMEM((LOCAL, LANES), F32),
            per_source,
            per_source,
            per_source,
            rim,
            rim,
            rim,
            rim,
            per_chunk,
            per_chunk,
            dense,
            pltpu.VMEM((SPEC, LANES), jnp.bfloat16),
            dense,
            per_chunk,
            per_source,
            per_source,
            pltpu.VMEM((ROWS, LOCAL, LANES), F32),
            dma((7,)),
            dma((LOCAL // SHARE,)),
            dma((2,)),
            dma((2,)),
            dma((4,)),
            dma((2,)),
            dma((9,)),
        ],
        compiler_params=pltpu.CompilerParams(
            collective_id=0, has_side_effects=True, vmem_limit_bytes=59 * 1024 * 1024
        ),
        cost_estimate=pl.CostEstimate(flops=2 * SPEC * SPEC * 256, bytes_accessed=16 << 20, transcendentals=0),
        name="exchange",
    )(spectrum, wind.reshape(2 * ROWS, LANES), sea_table, transfer_kernel, table, scalars)
    return result[: LOCAL * ROWS].reshape(LOCAL, ROWS, LANES)


def solution(mesh):
    placed = (P("comp", "region", None), P(None, "region", None), P("region", None), P())
    return jax.shard_map(
        on_device, mesh=mesh, in_specs=placed, out_specs=P("comp", "region", None), check_vma=False
    )
```

```python
import math

import jax
import jax.numpy as jnp
import numpy as np
from jax import lax
from jax.experimental import pallas as pl
from jax.experimental.pallas import tpu as pltpu
from jax.sharding import PartitionSpec as P

NDIR = 36
NFREQ = 48
SPEC = NDIR * NFREQ
COMPS = 64
LOCAL = SPEC // COMPS
REGIONS = 4
ROWS = 256
LANES = 128
BLOCKS = 64
STRIDE = ROWS + 16
PADDED_ROWS = ROWS + 8
PADDED_COMP = 32
PADDED_SPEC = SPEC + 32
TILE = 432
EARLY = 1
SHARE = 9
F32 = jnp.float32
MESH = pl.DeviceIdType.MESH

growth_rate = 0.05
wind_floor = 0.5
dissipation = 0.02
coupling = 0.5
courant_top = 0.6


def component_tables():
    comp = np.arange(SPEC)
    freq, direction = comp // NDIR, 2.0 * math.pi * (comp % NDIR + 0.5) / NDIR
    omega = 1.1 ** (freq - NFREQ // 2)
    speed = courant_top * 1.1 ** (-freq.astype(np.float64))
    cosine, sine = np.cos(direction), np.sin(direction)
    u, v = speed * cosine, speed * sine
    centre = 1.0 - np.abs(u) - np.abs(v)
    columns = [omega, cosine, sine, centre, np.maximum(u, 0), np.maximum(-u, 0), np.maximum(v, 0), np.maximum(-v, 0)]
    table = np.zeros((SPEC, LANES), np.float32)
    for lane, column in enumerate(columns):
        table[:, lane] = column
    scalars = np.zeros((COMPS, 8, LANES), np.float32)
    for row, column in enumerate([centre, np.abs(u), np.abs(v)]):
        scalars[:, row, :LOCAL] = column.reshape(COMPS, LOCAL)
    return table.reshape(COMPS, LOCAL, LANES), scalars


def energy_scale():
    return float(1.0 / (NDIR * np.sum(1.1 ** (np.arange(NFREQ) - NFREQ // 2.0))))


def shifted(me, step):
    z = ((me & 56) + (step & 56)) & 56
    y = ((me & 6) + (step & 6)) & 6
    return z + y + ((me + step) & 1)


def quarter_of(me, number):
    order = jnp.where(number == 2, 3, jnp.where(number == 3, 0, 2 - number))
    return ((me >> 4) + order) & 3


def device_in(me, quarter, place):
    return quarter * 16 + ((me ^ place ^ 8) & 8) + ((me + place) & 7)


def gathered(source, lanes):
    return jnp.take_along_axis(source, lanes, axis=1, mode="promise_in_bounds")


def spread_rows(row):
    return jnp.broadcast_to(row, (LOCAL, LANES))


def exchange_kernel(
    spectrum, wind_field, listed, transfer, table, scalars,
    result,
    wave0, wave1, wave2, sea_table, mask, sea_rows, lane_map, part_map, units, units_smem, scalars_smem,
    wind, kernel_buf, constants, own, omega, cosine, sine,
    to_west, to_east, from_west, from_east,
    outgoing, incoming, dense, rounded, coupled, returning, arrived_a, arrived_b, expanded,
    load_sem, comp_sem, halo_send, halo_recv, send_sem, forward_sem, back_sem,
):
    me = lax.axis_index("comp")
    region = lax.axis_index("region")
    west = (region + REGIONS - 1) & (REGIONS - 1)
    east = (region + 1) & (REGIONS - 1)

    def comp_load(comp):
        return pltpu.make_async_copy(
            spectrum.at[comp], wave0.at[pl.ds(comp * STRIDE + 8, ROWS)], comp_sem.at[comp // SHARE])

    barrier = pltpu.get_barrier_semaphore()

    for step in range(1, COMPS):
        pl.semaphore_signal(barrier, inc=1, device_id={"comp": shifted(me, step)}, device_id_type=MESH)
    pl.semaphore_signal(barrier, inc=1, device_id={"region": west}, device_id_type=MESH)
    pl.semaphore_signal(barrier, inc=1, device_id={"region": east}, device_id_type=MESH)

    load_listed = pltpu.make_async_copy(listed, sea_table, load_sem.at[6])
    load_listed.start()

    for comp in range(LOCAL):
        comp_load(comp).start()

    load_scalars = pltpu.make_async_copy(scalars.at[me], scalars_smem, load_sem.at[0])
    load_scalars.start()
    load_own = pltpu.make_async_copy(table.at[me], own, load_sem.at[1])
    load_own.start()
    load_constants = pltpu.make_async_copy(table, constants, load_sem.at[2])
    load_kernel = pltpu.make_async_copy(transfer, kernel_buf, load_sem.at[3])
    load_wind = pltpu.make_async_copy(wind_field, wind.at[pl.ds(0, 2 * ROWS)], load_sem.at[4])
    load_listed.wait()

    for part in range(4):
        sea_rows[pl.ds(part, BLOCKS, stride=4), :] = sea_table[:, part * LANES : (part + 1) * LANES]

    lane_number = lax.broadcasted_iota(jnp.int32, (LANES, 4 * LANES), 0)
    quarter = lax.broadcasted_iota(jnp.int32, (8, 4 * LANES), 0)

    def listed_maps(block, weights):
        cells = sea_table[pl.ds(block, 1), :]
        lane = jnp.where(cells >= 0, cells & (LANES - 1), -1)
        inside = jnp.where(cells >= 0, (cells >> 7) & 3, -1)
        match = jnp.where(lane == lane_number, 1.0, 0.0).astype(jnp.bfloat16)
        row = jnp.where(inside == quarter, 1.0, 0.0)
        rows = jnp.concatenate([row * w for w in weights], axis=0).astype(jnp.bfloat16)
        return lax.dot_general(rows, match, (((1,), (1,)), ((), ())), preferred_element_type=F32)

    def block_rows(block):
        return pl.ds(pl.multiple_of(block * 4, 4), 4)

    @pl.loop(0, BLOCKS, unroll=8)
    def _(block):
        mask[block_rows(block), :] = listed_maps(block, [1.0])[0:4]

    def strided(x):
        return pl.ds(x, LOCAL, stride=STRIDE)

    for share in range(LOCAL // SHARE):
        landed = wave0.at[pl.ds(0, SHARE * ROWS)]
        pltpu.make_async_copy(landed, landed, comp_sem.at[share]).wait()

        @pl.loop(share * SHARE, (share + 1) * SHARE)
        def _(comp):
            base = pl.multiple_of(comp * STRIDE + 8, 8)
            for start in range(0, ROWS, 64):
                rows = pl.ds(base + start, 64)
                wave0[rows, :] = mask[start : start + 64, :] * wave0[rows, :]

    nothing = jnp.zeros((LOCAL, LANES), F32)
    for wave in (wave0, wave1):
        wave[strided(7), :] = nothing
        wave[strided(8 + ROWS), :] = nothing

    first_row, last_row = wave0[strided(8), :], wave0[strided(7 + ROWS), :]
    to_west[0] = first_row
    to_west[1] = wave0[strided(9), :]
    to_west[2] = spread_rows(mask[0:1, :])
    to_east[0] = last_row
    to_east[1] = wave0[strided(6 + ROWS), :]
    to_east[2] = spread_rows(mask[ROWS - 1 : ROWS, :])
    pl.semaphore_wait(barrier, COMPS + 1)
    send_west = pltpu.make_async_remote_copy(
        to_west, from_east, halo_send.at[0], halo_recv.at[0], device_id={"region": west}, device_id_type=MESH)
    send_east = pltpu.make_async_remote_copy(
        to_east, from_west, halo_send.at[1], halo_recv.at[1], device_id={"region": east}, device_id_type=MESH)
    send_west.start()
    send_east.start()

    load_scalars.wait()
    lanes = lax.broadcasted_iota(jnp.int32, (8, LANES), 1)

    def substep(source, target, groups, unroll, origin=0):
        @pl.loop(0, LOCAL, unroll=unroll)
        def _(comp):
            direction = lax.rem(me * LOCAL + comp, NDIR)
            aside = jnp.where((direction < NDIR // 4) | (direction >= 3 * NDIR // 4), -1, 1)
            turn = jnp.where(direction < NDIR // 2, 1, LANES - 1)
            edge = jnp.where(direction < NDIR // 2, 0, LANES - 1)
            centre_w = jnp.full((8, LANES), scalars_smem[0, comp])
            x_w = jnp.full((8, LANES), scalars_smem[1, comp])
            y_w = jnp.where(lanes == edge, 0.0, scalars_smem[2, comp])
            for group in groups:
                row = pl.multiple_of(origin + 8 * group, 8)
                base = pl.multiple_of(comp * STRIDE + 8 + row, 8)
                here = source[pl.ds(base, 8), :]
                beside = source[pl.ds(base + aside, 8), :]
                changed = centre_w * here + x_w * beside + y_w * pltpu.roll(here, turn, 1)
                target[pl.ds(base, 8), :] = mask[pl.ds(row, 8), :] * changed

    first_quarter = quarter_of(me, 0)
    needed = jnp.clip(first_quarter * 64 - 8, 0, ROWS - 80)
    substep(wave0, wave1, range(10), 9, origin=needed)

    def packed(row):
        cells = sea_rows[pl.ds(row, 1), :]
        base = row & ~3
        lane = spread_rows(cells & (LANES - 1))
        inside = spread_rows((cells >> 7) & 3)
        total = gathered(wave2[strided(8 + base), :], lane)
        for number in range(1, 4):
            total = jnp.where(inside == number, gathered(wave2[strided(8 + base + number), :], lane), total)
        return total

    def unit_row(chunk, device):
        return jnp.clip(units_smem[0, device], 0, ROWS - 1) if chunk == 0 else device * 4

    def forward(chunk, target):
        return pltpu.make_async_remote_copy(
            outgoing.at[chunk, target], incoming.at[chunk, me], send_sem.at[chunk], forward_sem.at[chunk],
            device_id={"comp": target}, device_id_type=MESH)

    def send(chunk, target):
        outgoing[chunk, target] = packed(unit_row(chunk, target))
        forward(chunk, target).start()

    def quarter_sends(number):
        quarter = quarter_of(me, number)
        substep(wave1, wave2, range(8), 9, origin=quarter * 64)

        @pl.loop(0, 16)
        def _(place):
            target = device_in(me, quarter, place)
            ready = (target >= 4) & (target < BLOCKS - 4) if number == 0 else target != me

            @pl.when(ready)
            def _():
                send(1, target)

    quarter_sends(0)
    substep(wave0, wave1, range(ROWS // 8), 3)
    load_kernel.start()
    load_constants.start()
    load_wind.start()

    load_own.wait()
    coefficients = own[...]
    wide = lax.broadcasted_iota(jnp.int32, (LOCAL, LANES), 1)

    def column(number):
        return spread_rows(coefficients[:, number : number + 1])

    centre_w, west_w, east_w = column(3), column(4), column(5)
    south_w = jnp.where(wide == 0, 0.0, column(6))
    north_w = jnp.where(wide == LANES - 1, 0.0, column(7))

    def halo(rows, inside, outermost, before):
        near = jnp.where(inside, rows[0], 0.0)
        far = jnp.where(inside, rows[1], 0.0)
        sides = (far, outermost) if before else (outermost, far)
        changed = (
            centre_w * near + west_w * sides[0] + east_w * sides[1]
            + south_w * pltpu.roll(near, 1, 1) + north_w * pltpu.roll(near, LANES - 1, 1)
        )
        at = strided(7 if before else 8 + ROWS)
        wave0[at, :] = near
        wave1[at, :] = rows[2] * changed

    send_west.wait()
    send_east.wait()
    halo(from_west, region > 0, first_row, True)
    halo(from_east, region < REGIONS - 1, last_row, False)
    substep(wave0, wave1, (0, ROWS // 8 - 1), 9)
    substep(wave1, wave2, (0, ROWS // 8 - 1), 9)
    quarter_sends(1)

    row_number = lax.broadcasted_iota(jnp.int32, (ROWS, LANES), 0)
    lane_position = lax.broadcasted_iota(jnp.int32, (ROWS, LANES), 1)
    later = (sea_rows[0:ROWS, :] >= 0) & ((row_number & 3) > 0)
    count = jnp.where(later, 1.0, 0.0)
    lower = jnp.where(
        lax.broadcasted_iota(jnp.int32, (ROWS, ROWS), 0) > lax.broadcasted_iota(jnp.int32, (ROWS, ROWS), 1), 1.0, 0.0
    ).astype(jnp.bfloat16)
    rank = jnp.dot(lower, count.astype(jnp.bfloat16), preferred_element_type=F32)
    found = jnp.where((rank == lane_position.astype(F32)) & later, row_number.astype(F32), 0.0)
    before = jnp.where(row_number < lane_position * 4, count, 0.0)
    unit_rows = jnp.broadcast_to(jnp.sum(found, axis=0, keepdims=True), (4, LANES))
    first_units = jnp.broadcast_to(jnp.sum(before, axis=0, keepdims=True), (4, LANES))
    units[...] = jnp.concatenate([unit_rows, first_units], axis=0).astype(jnp.int32)
    load_units = pltpu.make_async_copy(units, units_smem, load_sem.at[5])
    load_units.start()

    quarter_sends(2)
    quarter_sends(3)

    @pl.when((first_quarter == 0) | (first_quarter == 3))
    def _():
        @pl.loop(0, 4)
        def _(place):
            send(1, first_quarter * 20 + ((me + place) & 3))

    load_units.wait()

    @pl.loop(0, 4)
    def _(number):
        quarter = quarter_of(me, number)

        @pl.loop(0, 16)
        def _(place):
            target = device_in(me, quarter, place)

            @pl.when(target != me)
            def _():
                send(0, target)

    for chunk in range(2):
        incoming[chunk, me] = packed(unit_row(chunk, me))

    load_constants.wait()

    @pl.loop(0, COMPS, unroll=4)
    def _(source):
        values = constants[source]
        omega[source] = spread_rows(values[:, 0:1])
        cosine[source] = spread_rows(values[:, 1:2])
        sine[source] = spread_rows(values[:, 2:3])

    slot = lax.broadcasted_iota(jnp.int32, (1, 4 * LANES), 1)
    slot_lane = (slot & (LANES - 1)).astype(F32)
    slot_part = (slot >> 7).astype(F32)

    @pl.loop(0, BLOCKS, unroll=8)
    def _(block):
        maps = listed_maps(block, [slot_lane, slot_part])
        rows = block_rows(block)
        lane_map[rows, :] = maps[0:4].astype(jnp.int32)
        part_map[rows, :] = jnp.where(mask[rows, :] > 0.5, maps[8:12], -1.0).astype(jnp.int32)

    load_kernel.wait()
    load_wind.wait()

    def wind_at(row):
        cells = sea_rows[pl.ds(row, 1), :]
        base = row & ~3
        lane = jnp.broadcast_to(cells & (LANES - 1), (8, LANES))
        inside = (cells >> 7) & 3
        parts = []
        for part in range(2):
            total = jnp.zeros((8, LANES), F32)
            for number in range(4):
                line = jnp.broadcast_to(wind[pl.ds(part * ROWS + base + number, 1), :], (8, LANES))
                total = jnp.where(inside == number, gathered(line, lane), total)
            parts.append(total[0:1])
        return parts

    def back(chunk, target, held):
        return pltpu.make_async_remote_copy(
            returning.at[chunk, target], held.at[me], send_sem.at[2 + chunk], back_sem.at[chunk, me >> 3],
            device_id={"comp": target}, device_id_type=MESH)

    def source_terms(chunk, held):
        landed = incoming.at[chunk, pl.ds(0, COMPS - 1)]
        pltpu.make_async_copy(landed, landed, forward_sem.at[chunk]).wait()
        wind_u, wind_v = wind_at(unit_row(chunk, me))

        def collect(source, total):
            values = incoming[chunk, source]
            dense[pl.ds(source * LOCAL, LOCAL), :] = values
            return total + omega[source] * values

        total = lax.fori_loop(0, COMPS, collect, jnp.zeros((LOCAL, LANES), F32), unroll=True)
        energy = jnp.sum(total, axis=0, keepdims=True) * energy_scale()
        loss = dissipation * energy * energy
        rounded[...] = dense[0:SPEC, :].astype(jnp.bfloat16)

        def updated(target):
            points = incoming[chunk, target]
            speed = omega[target]
            along = cosine[target] * wind_u + sine[target] * wind_v
            growth = growth_rate * speed * jnp.maximum(along - wind_floor, 0.0)
            damping = speed * speed * loss
            joined = coupled[pl.ds(target * LOCAL, LOCAL), :]
            return points + points * (growth - damping + coupling * joined) / (1.0 + damping)

        def update(number, sending):
            quarter = quarter_of(me, number)
            rows = pl.ds(pl.multiple_of(quarter * TILE, TILE), TILE)
            coupled[rows, :] = jnp.dot(kernel_buf[rows, :], rounded[...], preferred_element_type=F32)

            @pl.loop(0, 16, unroll=2)
            def _(place):
                target = device_in(me, quarter, place)
                values = updated(target)
                returning[chunk, target] = values

                @pl.when(target == me)
                def _():
                    held[me] = values

                if sending:

                    @pl.when(target != me)
                    def _():
                        back(chunk, target, held).start()

        return update

    update = source_terms(1, arrived_b)

    @pl.loop(0, EARLY)
    def _(number):
        update(number, True)

    @pl.loop(EARLY, 4)
    def _(number):
        update(number, False)

    update_later = source_terms(0, arrived_a)

    @pl.loop(0, 4)
    def _(number):
        update_later(number, True)

    @pl.loop(EARLY, 4)
    def _(number):
        quarter = quarter_of(me, number)

        @pl.loop(0, 16)
        def _(place):
            target = device_in(me, quarter, place)

            @pl.when(target != me)
            def _():
                back(1, target, arrived_b).start()

    def plane_of(number):
        shift = (4, 4, 2, 2, 6, 6, 0, 0)[number]
        return (((me >> 3) + 8 - shift) & 6) + (((me >> 3) + number + 1) & 1)

    def arrival(number, chunk, held):
        landed = held.at[pl.ds(0, 8 if number < 7 else 7)]
        pltpu.make_async_copy(landed, landed, back_sem.at[chunk, plane_of(number)]).wait()

    for number in range(8):
        arrival(number, 0, arrived_a)

        @pl.loop(0, 8, unroll=4)
        def _(place, number=number):
            unit = plane_of(number) * 8 + place
            base = jnp.clip(units_smem[0, unit], 0, ROWS - 1) & ~3
            values = arrived_a[unit]
            for line in range(4):
                lane = spread_rows(lane_map[pl.ds(base + line, 1), :])
                expanded[unit * 4 + line] = gathered(values, lane)

    def finish(block):
        values = arrived_b[block]
        first_unit = units_smem[4, block]
        for number in range(4):
            x = block * 4 + number
            line = pl.ds(x, 1)
            lane, part = spread_rows(lane_map[line, :]), spread_rows(part_map[line, :])
            piece = jnp.where(part == 0, gathered(values, lane), 0.0)
            for offset in range(3):
                unit = jnp.clip(first_unit + offset, 0, COMPS - 1)
                piece = jnp.where(part == offset + 1, expanded[unit * 4 + number], piece)
            result[pl.ds(x, LOCAL, stride=ROWS), :] = piece

    for number in range(8):
        arrival(number, 1, arrived_b)

        @pl.loop(0, 8, unroll=4)
        def _(place, number=number):
            finish(plane_of(number) * 8 + place)

    for number in range(4):
        sent = outgoing.at[0, pl.ds(0, COMPS - 1)]
        pltpu.make_async_copy(sent, sent, send_sem.at[number]).wait()


def on_device(spectrum, wind, sea_table, transfer_kernel):
    table, scalars = (jnp.asarray(array) for array in component_tables())
    anywhere = pl.BlockSpec(memory_space=pltpu.HBM)
    wave = pltpu.VMEM((PADDED_COMP * STRIDE, LANES), F32)
    line_map = pltpu.VMEM((PADDED_ROWS, LANES), jnp.int32)
    per_source = pltpu.VMEM((COMPS, LOCAL, LANES), F32)
    per_chunk = pltpu.VMEM((2, COMPS, LOCAL, LANES), F32)
    rim = pltpu.VMEM((3, LOCAL, LANES), F32)
    dense = pltpu.VMEM((PADDED_SPEC, LANES), F32)
    dma = pltpu.SemaphoreType.DMA
    result = pl.pallas_call(
        exchange_kernel,
        out_shape=pltpu.VMEM((PADDED_COMP * ROWS, LANES), F32),
        in_specs=[anywhere] * 6,
        out_specs=pl.BlockSpec(memory_space=pltpu.VMEM),
        scratch_shapes=[
            wave,
            wave,
            wave,
            pltpu.VMEM((BLOCKS, 4 * LANES), jnp.int32),
            pltpu.VMEM((PADDED_ROWS, LANES), F32),
            line_map,
            line_map,
            line_map,
            pltpu.VMEM((8, LANES), jnp.int32),
            pltpu.SMEM((8, LANES), jnp.int32),
            pltpu.SMEM((8, LANES), F32),
            pltpu.VMEM((2 * ROWS + 8, LANES), F32),
            pltpu.VMEM((SPEC, SPEC), jnp.bfloat16),
            per_source,
            pltpu.VMEM((LOCAL, LANES), F32),
            per_source,
            per_source,
            per_source,
            rim,
            rim,
            rim,
            rim,
            per_chunk,
            per_chunk,
            dense,
            pltpu.VMEM((SPEC, LANES), jnp.bfloat16),
            dense,
            per_chunk,
            per_source,
            per_source,
            pltpu.VMEM((ROWS, LOCAL, LANES), F32),
            dma((7,)),
            dma((LOCAL // SHARE,)),
            dma((2,)),
            dma((2,)),
            dma((4,)),
            dma((2,)),
            dma((2, 8)),
        ],
        compiler_params=pltpu.CompilerParams(
            collective_id=0, has_side_effects=True, vmem_limit_bytes=59 * 1024 * 1024
        ),
        cost_estimate=pl.CostEstimate(flops=2 * SPEC * SPEC * 256, bytes_accessed=16 << 20, transcendentals=0),
        name="exchange",
    )(spectrum, wind.reshape(2 * ROWS, LANES), sea_table, transfer_kernel, table, scalars)
    return result[: LOCAL * ROWS].reshape(LOCAL, ROWS, LANES)


def solution(mesh):
    placed = (P("comp", "region", None), P(None, "region", None), P("region", None), P())
    return jax.shard_map(
        on_device, mesh=mesh, in_specs=placed, out_specs=P("comp", "region", None), check_vma=False
    )
```

```python
import math

import jax
import jax.numpy as jnp
import numpy as np
from jax import lax
from jax.experimental import pallas as pl
from jax.experimental.pallas import tpu as pltpu
from jax.sharding import PartitionSpec as P

NDIR = 36
NFREQ = 48
SPEC = NDIR * NFREQ
COMPS = 64
LOCAL = SPEC // COMPS
REGIONS = 4
ROWS = 256
LANES = 128
BLOCKS = 64
STRIDE = ROWS + 16
PADDED_ROWS = ROWS + 8
PADDED_COMP = 32
PADDED_SPEC = SPEC + 32
TILE = 432
EARLY = 1
SHARE = 9
F32 = jnp.float32
MESH = pl.DeviceIdType.MESH

growth_rate = 0.05
wind_floor = 0.5
dissipation = 0.02
coupling = 0.5
courant_top = 0.6


def component_tables():
    comp = np.arange(SPEC)
    freq, direction = comp // NDIR, 2.0 * math.pi * (comp % NDIR + 0.5) / NDIR
    omega = 1.1 ** (freq - NFREQ // 2)
    speed = courant_top * 1.1 ** (-freq.astype(np.float64))
    cosine, sine = np.cos(direction), np.sin(direction)
    u, v = speed * cosine, speed * sine
    centre = 1.0 - np.abs(u) - np.abs(v)
    columns = [omega, cosine, sine, centre, np.maximum(u, 0), np.maximum(-u, 0), np.maximum(v, 0), np.maximum(-v, 0)]
    table = np.zeros((SPEC, LANES), np.float32)
    for lane, column in enumerate(columns):
        table[:, lane] = column
    scalars = np.zeros((COMPS, 8, LANES), np.float32)
    for row, column in enumerate([centre, np.abs(u), np.abs(v)]):
        scalars[:, row, :LOCAL] = column.reshape(COMPS, LOCAL)
    return table.reshape(COMPS, LOCAL, LANES), scalars


def energy_scale():
    return float(1.0 / (NDIR * np.sum(1.1 ** (np.arange(NFREQ) - NFREQ // 2.0))))


def shifted(me, step):
    z = ((me & 56) + (step & 56)) & 56
    y = ((me & 6) + (step & 6)) & 6
    return z + y + ((me + step) & 1)


def quarter_of(me, number):
    order = jnp.where(number == 2, 3, jnp.where(number == 3, 0, 2 - number))
    return ((me >> 4) + order) & 3


def device_in(me, quarter, place):
    return quarter * 16 + ((me ^ place ^ 8) & 8) + ((me + place) & 7)


def gathered(source, lanes):
    return jnp.take_along_axis(source, lanes, axis=1, mode="promise_in_bounds")


def spread_rows(row):
    return jnp.broadcast_to(row, (LOCAL, LANES))


def exchange_kernel(
    spectrum, wind_field, listed, transfer, table, scalars,
    result,
    wave0, wave1, wave2, sea_table, mask, sea_rows, lane_map, part_map, units, units_smem, scalars_smem,
    wind, kernel_buf, constants, own, omega, cosine, sine,
    to_west, to_east, from_west, from_east,
    outgoing, incoming, dense, rounded, coupled, returning, arrived_a, arrived_b, expanded,
    load_sem, comp_sem, halo_send, halo_recv, send_sem, forward_sem, back_sem,
):
    me = lax.axis_index("comp")
    region = lax.axis_index("region")
    west = (region + REGIONS - 1) & (REGIONS - 1)
    east = (region + 1) & (REGIONS - 1)

    def comp_load(comp):
        return pltpu.make_async_copy(
            spectrum.at[comp], wave0.at[pl.ds(comp * STRIDE + 8, ROWS)], comp_sem.at[comp // SHARE])

    barrier = pltpu.get_barrier_semaphore()

    for step in range(1, COMPS):
        pl.semaphore_signal(barrier, inc=1, device_id={"comp": shifted(me, step)}, device_id_type=MESH)
    pl.semaphore_signal(barrier, inc=1, device_id={"region": west}, device_id_type=MESH)
    pl.semaphore_signal(barrier, inc=1, device_id={"region": east}, device_id_type=MESH)

    load_listed = pltpu.make_async_copy(listed, sea_table, load_sem.at[6])
    load_listed.start()

    for comp in range(LOCAL):
        comp_load(comp).start()

    load_scalars = pltpu.make_async_copy(scalars.at[me], scalars_smem, load_sem.at[0])
    load_scalars.start()
    load_own = pltpu.make_async_copy(table.at[me], own, load_sem.at[1])
    load_own.start()
    load_constants = pltpu.make_async_copy(table, constants, load_sem.at[2])
    load_kernel = pltpu.make_async_copy(transfer, kernel_buf, load_sem.at[3])
    load_wind = pltpu.make_async_copy(wind_field, wind.at[pl.ds(0, 2 * ROWS)], load_sem.at[4])
    load_listed.wait()

    for part in range(4):
        sea_rows[pl.ds(part, BLOCKS, stride=4), :] = sea_table[:, part * LANES : (part + 1) * LANES]

    lane_number = lax.broadcasted_iota(jnp.int32, (LANES, 4 * LANES), 0)
    quarter = lax.broadcasted_iota(jnp.int32, (8, 4 * LANES), 0)

    def listed_maps(block, weights):
        cells = sea_table[pl.ds(block, 1), :]
        lane = jnp.where(cells >= 0, cells & (LANES - 1), -1)
        inside = jnp.where(cells >= 0, (cells >> 7) & 3, -1)
        match = jnp.where(lane == lane_number, 1.0, 0.0).astype(jnp.bfloat16)
        row = jnp.where(inside == quarter, 1.0, 0.0)
        rows = jnp.concatenate([row * w for w in weights], axis=0).astype(jnp.bfloat16)
        return lax.dot_general(rows, match, (((1,), (1,)), ((), ())), preferred_element_type=F32)

    def block_rows(block):
        return pl.ds(pl.multiple_of(block * 4, 4), 4)

    def mask_block(block):
        mask[block_rows(block), :] = listed_maps(block, [1.0])[0:4]

    def strided(x):
        return pl.ds(x, LOCAL, stride=STRIDE)

    def masked(comp, start, count):
        rows = pl.ds(pl.multiple_of(comp * STRIDE + 8 + start, 8), count)
        wave0[rows, :] = mask[pl.ds(pl.multiple_of(start, 8), count), :] * wave0[rows, :]

    first_quarter = quarter_of(me, 0)

    def rows_for(number):
        return jnp.clip(quarter_of(me, number) * 64 - 8, 0, ROWS - 80)

    def quarter_mask(number):
        @pl.loop(0, 20, unroll=10)
        def _(place):
            mask_block((rows_for(number) >> 2) + place)

    quarter_mask(0)
    for block in (0, 1, BLOCKS - 2, BLOCKS - 1):
        mask_block(block)

    for share in range(LOCAL // SHARE):
        landed = wave0.at[pl.ds(0, SHARE * ROWS)]
        pltpu.make_async_copy(landed, landed, comp_sem.at[share]).wait()

        @pl.loop(share * SHARE, (share + 1) * SHARE, unroll=3)
        def _(comp):
            masked(comp, rows_for(0), 80)
            masked(comp, 0, 8)
            masked(comp, ROWS - 8, 8)

    nothing = jnp.zeros((LOCAL, LANES), F32)
    for wave in (wave0, wave1):
        wave[strided(7), :] = nothing
        wave[strided(8 + ROWS), :] = nothing

    first_row, last_row = wave0[strided(8), :], wave0[strided(7 + ROWS), :]
    to_west[0] = first_row
    to_west[1] = wave0[strided(9), :]
    to_west[2] = spread_rows(mask[0:1, :])
    to_east[0] = last_row
    to_east[1] = wave0[strided(6 + ROWS), :]
    to_east[2] = spread_rows(mask[ROWS - 1 : ROWS, :])
    load_scalars.wait()
    lanes = lax.broadcasted_iota(jnp.int32, (8, LANES), 1)

    def substep(source, target, groups, unroll, origin=0):
        @pl.loop(0, LOCAL, unroll=unroll)
        def _(comp):
            direction = lax.rem(me * LOCAL + comp, NDIR)
            aside = jnp.where((direction < NDIR // 4) | (direction >= 3 * NDIR // 4), -1, 1)
            turn = jnp.where(direction < NDIR // 2, 1, LANES - 1)
            edge = jnp.where(direction < NDIR // 2, 0, LANES - 1)
            centre_w = jnp.full((8, LANES), scalars_smem[0, comp])
            x_w = jnp.full((8, LANES), scalars_smem[1, comp])
            y_w = jnp.where(lanes == edge, 0.0, scalars_smem[2, comp])
            for group in groups:
                row = pl.multiple_of(origin + 8 * group, 8)
                base = pl.multiple_of(comp * STRIDE + 8 + row, 8)
                here = source[pl.ds(base, 8), :]
                beside = source[pl.ds(base + aside, 8), :]
                changed = centre_w * here + x_w * beside + y_w * pltpu.roll(here, turn, 1)
                target[pl.ds(base, 8), :] = mask[pl.ds(row, 8), :] * changed

    substep(wave0, wave1, range(10), 9, origin=rows_for(0))

    def packed(row):
        cells = sea_rows[pl.ds(row, 1), :]
        base = row & ~3
        lane = spread_rows(cells & (LANES - 1))
        inside = spread_rows((cells >> 7) & 3)
        total = gathered(wave2[strided(8 + base), :], lane)
        for number in range(1, 4):
            total = jnp.where(inside == number, gathered(wave2[strided(8 + base + number), :], lane), total)
        return total

    def unit_row(chunk, device):
        return jnp.clip(units_smem[0, device], 0, ROWS - 1) if chunk == 0 else device * 4

    def forward(chunk, target):
        return pltpu.make_async_remote_copy(
            outgoing.at[chunk, target], incoming.at[chunk, me], send_sem.at[chunk], forward_sem.at[chunk],
            device_id={"comp": target}, device_id_type=MESH)

    def send(chunk, target):
        outgoing[chunk, target] = packed(unit_row(chunk, target))
        forward(chunk, target).start()

    def quarter_step(number):
        substep(wave1, wave2, range(8), 9, origin=quarter_of(me, number) * 64)

    def quarter_sends(number):
        quarter = quarter_of(me, number)

        @pl.loop(0, 16)
        def _(place):
            target = device_in(me, quarter, place)
            ready = (target >= 4) & (target < BLOCKS - 4) if number == 0 else target != me

            @pl.when(ready)
            def _():
                send(1, target)

    quarter_step(0)
    pl.semaphore_wait(barrier, COMPS + 1)
    send_west = pltpu.make_async_remote_copy(
        to_west, from_east, halo_send.at[0], halo_recv.at[0], device_id={"region": west}, device_id_type=MESH)
    send_east = pltpu.make_async_remote_copy(
        to_east, from_west, halo_send.at[1], halo_recv.at[1], device_id={"region": east}, device_id_type=MESH)
    send_west.start()
    send_east.start()

    quarter_sends(0)

    def prepare(number):
        quarter_mask(number)

        @pl.loop(0, LOCAL, unroll=3)
        def _(comp):
            masked(comp, rows_for(number), 80)

        substep(wave0, wave1, range(10), 9, origin=rows_for(number))

    prepare(1)
    load_kernel.start()
    load_constants.start()
    load_wind.start()

    load_own.wait()
    coefficients = own[...]
    wide = lax.broadcasted_iota(jnp.int32, (LOCAL, LANES), 1)

    def column(number):
        return spread_rows(coefficients[:, number : number + 1])

    centre_w, west_w, east_w = column(3), column(4), column(5)
    south_w = jnp.where(wide == 0, 0.0, column(6))
    north_w = jnp.where(wide == LANES - 1, 0.0, column(7))

    def halo(rows, inside, outermost, before):
        near = jnp.where(inside, rows[0], 0.0)
        far = jnp.where(inside, rows[1], 0.0)
        sides = (far, outermost) if before else (outermost, far)
        changed = (
            centre_w * near + west_w * sides[0] + east_w * sides[1]
            + south_w * pltpu.roll(near, 1, 1) + north_w * pltpu.roll(near, LANES - 1, 1)
        )
        at = strided(7 if before else 8 + ROWS)
        wave0[at, :] = near
        wave1[at, :] = rows[2] * changed

    send_west.wait()
    send_east.wait()
    halo(from_west, region > 0, first_row, True)
    halo(from_east, region < REGIONS - 1, last_row, False)
    substep(wave0, wave1, (0, ROWS // 8 - 1), 9)
    substep(wave1, wave2, (0, ROWS // 8 - 1), 9)
    quarter_step(1)
    quarter_sends(1)

    row_number = lax.broadcasted_iota(jnp.int32, (ROWS, LANES), 0)
    lane_position = lax.broadcasted_iota(jnp.int32, (ROWS, LANES), 1)
    later = (sea_rows[0:ROWS, :] >= 0) & ((row_number & 3) > 0)
    count = jnp.where(later, 1.0, 0.0)
    lower = jnp.where(
        lax.broadcasted_iota(jnp.int32, (ROWS, ROWS), 0) > lax.broadcasted_iota(jnp.int32, (ROWS, ROWS), 1), 1.0, 0.0
    ).astype(jnp.bfloat16)
    rank = jnp.dot(lower, count.astype(jnp.bfloat16), preferred_element_type=F32)
    found = jnp.where((rank == lane_position.astype(F32)) & later, row_number.astype(F32), 0.0)
    before = jnp.where(row_number < lane_position * 4, count, 0.0)
    unit_rows = jnp.broadcast_to(jnp.sum(found, axis=0, keepdims=True), (4, LANES))
    first_units = jnp.broadcast_to(jnp.sum(before, axis=0, keepdims=True), (4, LANES))
    units[...] = jnp.concatenate([unit_rows, first_units], axis=0).astype(jnp.int32)
    load_units = pltpu.make_async_copy(units, units_smem, load_sem.at[5])
    load_units.start()

    prepare(2)
    quarter_step(2)
    quarter_sends(2)
    prepare(3)
    quarter_step(3)
    quarter_sends(3)

    @pl.when((first_quarter == 0) | (first_quarter == 3))
    def _():
        @pl.loop(0, 4)
        def _(place):
            send(1, first_quarter * 20 + ((me + place) & 3))

    load_units.wait()

    @pl.loop(0, 4)
    def _(number):
        quarter = quarter_of(me, number)

        @pl.loop(0, 16)
        def _(place):
            target = device_in(me, quarter, place)

            @pl.when(target != me)
            def _():
                send(0, target)

    for chunk in range(2):
        incoming[chunk, me] = packed(unit_row(chunk, me))

    load_constants.wait()

    @pl.loop(0, COMPS, unroll=4)
    def _(source):
        values = constants[source]
        omega[source] = spread_rows(values[:, 0:1])
        cosine[source] = spread_rows(values[:, 1:2])
        sine[source] = spread_rows(values[:, 2:3])

    slot = lax.broadcasted_iota(jnp.int32, (1, 4 * LANES), 1)
    slot_lane = (slot & (LANES - 1)).astype(F32)
    slot_part = (slot >> 7).astype(F32)

    @pl.loop(0, BLOCKS, unroll=8)
    def _(block):
        maps = listed_maps(block, [slot_lane, slot_part])
        rows = block_rows(block)
        lane_map[rows, :] = maps[0:4].astype(jnp.int32)
        part_map[rows, :] = jnp.where(mask[rows, :] > 0.5, maps[8:12], -1.0).astype(jnp.int32)

    load_kernel.wait()
    load_wind.wait()

    def wind_at(row):
        cells = sea_rows[pl.ds(row, 1), :]
        base = row & ~3
        lane = jnp.broadcast_to(cells & (LANES - 1), (8, LANES))
        inside = (cells >> 7) & 3
        parts = []
        for part in range(2):
            total = jnp.zeros((8, LANES), F32)
            for number in range(4):
                line = jnp.broadcast_to(wind[pl.ds(part * ROWS + base + number, 1), :], (8, LANES))
                total = jnp.where(inside == number, gathered(line, lane), total)
            parts.append(total[0:1])
        return parts

    def back(chunk, target, held):
        return pltpu.make_async_remote_copy(
            returning.at[chunk, target], held.at[me], send_sem.at[2 + chunk], back_sem.at[chunk, me >> 3],
            device_id={"comp": target}, device_id_type=MESH)

    def source_terms(chunk, held):
        landed = incoming.at[chunk, pl.ds(0, COMPS - 1)]
        pltpu.make_async_copy(landed, landed, forward_sem.at[chunk]).wait()
        wind_u, wind_v = wind_at(unit_row(chunk, me))

        def collect(source, total):
            values = incoming[chunk, source]
            dense[pl.ds(source * LOCAL, LOCAL), :] = values
            return total + omega[source] * values

        total = lax.fori_loop(0, COMPS, collect, jnp.zeros((LOCAL, LANES), F32), unroll=True)
        energy = jnp.sum(total, axis=0, keepdims=True) * energy_scale()
        loss = dissipation * energy * energy
        rounded[...] = dense[0:SPEC, :].astype(jnp.bfloat16)

        def updated(target):
            points = incoming[chunk, target]
            speed = omega[target]
            along = cosine[target] * wind_u + sine[target] * wind_v
            growth = growth_rate * speed * jnp.maximum(along - wind_floor, 0.0)
            damping = speed * speed * loss
            joined = coupled[pl.ds(target * LOCAL, LOCAL), :]
            return points + points * (growth - damping + coupling * joined) / (1.0 + damping)

        def update(number, sending):
            quarter = quarter_of(me, number)
            rows = pl.ds(pl.multiple_of(quarter * TILE, TILE), TILE)
            coupled[rows, :] = jnp.dot(kernel_buf[rows, :], rounded[...], preferred_element_type=F32)

            @pl.loop(0, 16, unroll=2)
            def _(place):
                target = device_in(me, quarter, place)
                values = updated(target)
                returning[chunk, target] = values

                @pl.when(target == me)
                def _():
                    held[me] = values

                if sending:

                    @pl.when(target != me)
                    def _():
                        back(chunk, target, held).start()

        return update

    update = source_terms(1, arrived_b)

    @pl.loop(0, EARLY)
    def _(number):
        update(number, True)

    @pl.loop(EARLY, 4)
    def _(number):
        update(number, False)

    update_later = source_terms(0, arrived_a)

    @pl.loop(0, 4)
    def _(number):
        update_later(number, True)

    @pl.loop(EARLY, 4)
    def _(number):
        quarter = quarter_of(me, number)

        @pl.loop(0, 16)
        def _(place):
            target = device_in(me, quarter, place)

            @pl.when(target != me)
            def _():
                back(1, target, arrived_b).start()

    def plane_of(number):
        shift = (4, 4, 2, 2, 6, 6, 0, 0)[number]
        return (((me >> 3) + 8 - shift) & 6) + (((me >> 3) + number + 1) & 1)

    def arrival(number, chunk, held):
        landed = held.at[pl.ds(0, 8 if number < 7 else 7)]
        pltpu.make_async_copy(landed, landed, back_sem.at[chunk, plane_of(number)]).wait()

    for number in range(8):
        arrival(number, 0, arrived_a)

        @pl.loop(0, 8, unroll=4)
        def _(place, number=number):
            unit = plane_of(number) * 8 + place
            base = jnp.clip(units_smem[0, unit], 0, ROWS - 1) & ~3
            values = arrived_a[unit]
            for line in range(4):
                lane = spread_rows(lane_map[pl.ds(base + line, 1), :])
                expanded[unit * 4 + line] = gathered(values, lane)

    def finish(block):
        values = arrived_b[block]
        first_unit = units_smem[4, block]
        for number in range(4):
            x = block * 4 + number
            line = pl.ds(x, 1)
            lane, part = spread_rows(lane_map[line, :]), spread_rows(part_map[line, :])
            piece = jnp.where(part == 0, gathered(values, lane), 0.0)
            for offset in range(3):
                unit = jnp.clip(first_unit + offset, 0, COMPS - 1)
                piece = jnp.where(part == offset + 1, expanded[unit * 4 + number], piece)
            result[pl.ds(x, LOCAL, stride=ROWS), :] = piece

    for number in range(8):
        arrival(number, 1, arrived_b)

        @pl.loop(0, 8, unroll=4)
        def _(place, number=number):
            finish(plane_of(number) * 8 + place)

    for number in range(4):
        sent = outgoing.at[0, pl.ds(0, COMPS - 1)]
        pltpu.make_async_copy(sent, sent, send_sem.at[number]).wait()


def on_device(spectrum, wind, sea_table, transfer_kernel):
    table, scalars = (jnp.asarray(array) for array in component_tables())
    anywhere = pl.BlockSpec(memory_space=pltpu.HBM)
    wave = pltpu.VMEM((PADDED_COMP * STRIDE, LANES), F32)
    line_map = pltpu.VMEM((PADDED_ROWS, LANES), jnp.int32)
    per_source = pltpu.VMEM((COMPS, LOCAL, LANES), F32)
    per_chunk = pltpu.VMEM((2, COMPS, LOCAL, LANES), F32)
    rim = pltpu.VMEM((3, LOCAL, LANES), F32)
    dense = pltpu.VMEM((PADDED_SPEC, LANES), F32)
    dma = pltpu.SemaphoreType.DMA
    result = pl.pallas_call(
        exchange_kernel,
        out_shape=pltpu.VMEM((PADDED_COMP * ROWS, LANES), F32),
        in_specs=[anywhere] * 6,
        out_specs=pl.BlockSpec(memory_space=pltpu.VMEM),
        scratch_shapes=[
            wave,
            wave,
            wave,
            pltpu.VMEM((BLOCKS, 4 * LANES), jnp.int32),
            pltpu.VMEM((PADDED_ROWS, LANES), F32),
            line_map,
            line_map,
            line_map,
            pltpu.VMEM((8, LANES), jnp.int32),
            pltpu.SMEM((8, LANES), jnp.int32),
            pltpu.SMEM((8, LANES), F32),
            pltpu.VMEM((2 * ROWS + 8, LANES), F32),
            pltpu.VMEM((SPEC, SPEC), jnp.bfloat16),
            per_source,
            pltpu.VMEM((LOCAL, LANES), F32),
            per_source,
            per_source,
            per_source,
            rim,
            rim,
            rim,
            rim,
            per_chunk,
            per_chunk,
            dense,
            pltpu.VMEM((SPEC, LANES), jnp.bfloat16),
            dense,
            per_chunk,
            per_source,
            per_source,
            pltpu.VMEM((ROWS, LOCAL, LANES), F32),
            dma((7,)),
            dma((LOCAL // SHARE,)),
            dma((2,)),
            dma((2,)),
            dma((4,)),
            dma((2,)),
            dma((2, 8)),
        ],
        compiler_params=pltpu.CompilerParams(
            collective_id=0, has_side_effects=True, vmem_limit_bytes=59 * 1024 * 1024
        ),
        cost_estimate=pl.CostEstimate(flops=2 * SPEC * SPEC * 256, bytes_accessed=16 << 20, transcendentals=0),
        name="exchange",
    )(spectrum, wind.reshape(2 * ROWS, LANES), sea_table, transfer_kernel, table, scalars)
    return result[: LOCAL * ROWS].reshape(LOCAL, ROWS, LANES)


def solution(mesh):
    placed = (P("comp", "region", None), P(None, "region", None), P("region", None), P())
    return jax.shard_map(
        on_device, mesh=mesh, in_specs=placed, out_specs=P("comp", "region", None), check_vma=False
    )
```

```python
import math

import jax
import jax.numpy as jnp
import numpy as np
from jax import lax
from jax.experimental import pallas as pl
from jax.experimental.pallas import tpu as pltpu
from jax.sharding import PartitionSpec as P

NDIR = 36
NFREQ = 48
SPEC = NDIR * NFREQ
COMPS = 64
LOCAL = SPEC // COMPS
REGIONS = 4
ROWS = 256
LANES = 128
BLOCKS = 64
STRIDE = ROWS + 16
PADDED_ROWS = ROWS + 8
PADDED_COMP = 32
PADDED_SPEC = SPEC + 32
TILE = 432
EARLY = 1
SHARE = 9
F32 = jnp.float32
MESH = pl.DeviceIdType.MESH

growth_rate = 0.05
wind_floor = 0.5
dissipation = 0.02
coupling = 0.5
courant_top = 0.6


def component_tables():
    comp = np.arange(SPEC)
    freq, direction = comp // NDIR, 2.0 * math.pi * (comp % NDIR + 0.5) / NDIR
    omega = 1.1 ** (freq - NFREQ // 2)
    speed = courant_top * 1.1 ** (-freq.astype(np.float64))
    cosine, sine = np.cos(direction), np.sin(direction)
    u, v = speed * cosine, speed * sine
    centre = 1.0 - np.abs(u) - np.abs(v)
    columns = [omega, cosine, sine, centre, np.maximum(u, 0), np.maximum(-u, 0), np.maximum(v, 0), np.maximum(-v, 0)]
    table = np.zeros((SPEC, LANES), np.float32)
    for lane, column in enumerate(columns):
        table[:, lane] = column
    scalars = np.zeros((COMPS, 8, LANES), np.float32)
    for row, column in enumerate([centre, np.abs(u), np.abs(v)]):
        scalars[:, row, :LOCAL] = column.reshape(COMPS, LOCAL)
    return table.reshape(COMPS, LOCAL, LANES), scalars


def energy_scale():
    return float(1.0 / (NDIR * np.sum(1.1 ** (np.arange(NFREQ) - NFREQ // 2.0))))


def shifted(me, step):
    z = ((me & 56) + (step & 56)) & 56
    y = ((me & 6) + (step & 6)) & 6
    return z + y + ((me + step) & 1)


def quarter_of(me, number):
    order = jnp.where(number == 2, 3, jnp.where(number == 3, 0, 2 - number))
    return ((me >> 4) + order) & 3


def device_in(me, quarter, place):
    return quarter * 16 + ((me ^ place ^ 8) & 8) + ((me + place) & 7)


def gathered(source, lanes):
    return jnp.take_along_axis(source, lanes, axis=1, mode="promise_in_bounds")


def spread_rows(row):
    return jnp.broadcast_to(row, (LOCAL, LANES))


def exchange_kernel(
    spectrum, wind_field, listed, transfer, table, scalars,
    result,
    wave0, wave1, wave2, sea_table, mask, sea_rows, lane_map, part_map, units, units_smem, scalars_smem,
    wind, kernel_buf, constants, own, omega, cosine, sine,
    to_west, to_east, from_west, from_east,
    outgoing, incoming, dense, rounded, coupled, returning, arrived_a, arrived_b, expanded,
    load_sem, comp_sem, halo_send, halo_recv, send_sem, forward_sem, back_sem,
):
    me = lax.axis_index("comp")
    region = lax.axis_index("region")
    west = (region + REGIONS - 1) & (REGIONS - 1)
    east = (region + 1) & (REGIONS - 1)

    def comp_load(comp):
        return pltpu.make_async_copy(
            spectrum.at[comp], wave0.at[pl.ds(comp * STRIDE + 8, ROWS)], comp_sem.at[comp // SHARE])

    barrier = pltpu.get_barrier_semaphore()

    for step in range(1, COMPS):
        pl.semaphore_signal(barrier, inc=1, device_id={"comp": shifted(me, step)}, device_id_type=MESH)
    pl.semaphore_signal(barrier, inc=1, device_id={"region": west}, device_id_type=MESH)
    pl.semaphore_signal(barrier, inc=1, device_id={"region": east}, device_id_type=MESH)

    load_listed = pltpu.make_async_copy(listed, sea_table, load_sem.at[6])
    load_listed.start()

    for comp in range(LOCAL):
        comp_load(comp).start()

    load_scalars = pltpu.make_async_copy(scalars.at[me], scalars_smem, load_sem.at[0])
    load_scalars.start()
    load_own = pltpu.make_async_copy(table.at[me], own, load_sem.at[1])
    load_own.start()
    load_constants = pltpu.make_async_copy(table, constants, load_sem.at[2])
    load_kernel = pltpu.make_async_copy(transfer, kernel_buf, load_sem.at[3])
    load_wind = pltpu.make_async_copy(wind_field, wind.at[pl.ds(0, 2 * ROWS)], load_sem.at[4])
    load_listed.wait()

    for part in range(4):
        sea_rows[pl.ds(part, BLOCKS, stride=4), :] = sea_table[:, part * LANES : (part + 1) * LANES]

    lane_number = lax.broadcasted_iota(jnp.int32, (LANES, 4 * LANES), 0)
    quarter = lax.broadcasted_iota(jnp.int32, (8, 4 * LANES), 0)

    def listed_maps(block, weights):
        cells = sea_table[pl.ds(block, 1), :]
        lane = jnp.where(cells >= 0, cells & (LANES - 1), -1)
        inside = jnp.where(cells >= 0, (cells >> 7) & 3, -1)
        match = jnp.where(lane == lane_number, 1.0, 0.0).astype(jnp.bfloat16)
        row = jnp.where(inside == quarter, 1.0, 0.0)
        rows = jnp.concatenate([row * w for w in weights], axis=0).astype(jnp.bfloat16)
        return lax.dot_general(rows, match, (((1,), (1,)), ((), ())), preferred_element_type=F32)

    def block_rows(block):
        return pl.ds(pl.multiple_of(block * 4, 4), 4)

    def mask_block(block):
        mask[block_rows(block), :] = listed_maps(block, [1.0])[0:4]

    def strided(x):
        return pl.ds(x, LOCAL, stride=STRIDE)

    def masked(comp, start, count):
        rows = pl.ds(pl.multiple_of(comp * STRIDE + 8 + start, 8), count)
        wave0[rows, :] = mask[pl.ds(pl.multiple_of(start, 8), count), :] * wave0[rows, :]

    first_quarter = quarter_of(me, 0)

    def rows_for(number):
        return jnp.clip(quarter_of(me, number) * 64 - 8, 0, ROWS - 80)

    def quarter_mask(number):
        @pl.loop(0, 20, unroll=10)
        def _(place):
            mask_block((rows_for(number) >> 2) + place)

    quarter_mask(0)
    for block in (0, 1, BLOCKS - 2, BLOCKS - 1):
        mask_block(block)

    for share in range(LOCAL // SHARE):
        landed = wave0.at[pl.ds(0, SHARE * ROWS)]
        pltpu.make_async_copy(landed, landed, comp_sem.at[share]).wait()

        @pl.loop(share * SHARE, (share + 1) * SHARE, unroll=3)
        def _(comp):
            masked(comp, rows_for(0), 80)
            masked(comp, 0, 8)
            masked(comp, ROWS - 8, 8)

    nothing = jnp.zeros((LOCAL, LANES), F32)
    for wave in (wave0, wave1):
        wave[strided(7), :] = nothing
        wave[strided(8 + ROWS), :] = nothing

    first_row, last_row = wave0[strided(8), :], wave0[strided(7 + ROWS), :]
    to_west[0] = first_row
    to_west[1] = wave0[strided(9), :]
    to_west[2] = spread_rows(mask[0:1, :])
    to_east[0] = last_row
    to_east[1] = wave0[strided(6 + ROWS), :]
    to_east[2] = spread_rows(mask[ROWS - 1 : ROWS, :])
    load_scalars.wait()
    lanes = lax.broadcasted_iota(jnp.int32, (8, LANES), 1)

    def substep(source, target, groups, unroll, origin=0):
        @pl.loop(0, LOCAL, unroll=unroll)
        def _(comp):
            direction = lax.rem(me * LOCAL + comp, NDIR)
            aside = jnp.where((direction < NDIR // 4) | (direction >= 3 * NDIR // 4), -1, 1)
            turn = jnp.where(direction < NDIR // 2, 1, LANES - 1)
            edge = jnp.where(direction < NDIR // 2, 0, LANES - 1)
            centre_w = jnp.full((8, LANES), scalars_smem[0, comp])
            x_w = jnp.full((8, LANES), scalars_smem[1, comp])
            y_w = jnp.where(lanes == edge, 0.0, scalars_smem[2, comp])
            for group in groups:
                row = pl.multiple_of(origin + 8 * group, 8)
                base = pl.multiple_of(comp * STRIDE + 8 + row, 8)
                here = source[pl.ds(base, 8), :]
                beside = source[pl.ds(base + aside, 8), :]
                changed = centre_w * here + x_w * beside + y_w * pltpu.roll(here, turn, 1)
                target[pl.ds(base, 8), :] = mask[pl.ds(row, 8), :] * changed

    substep(wave0, wave1, range(10), 9, origin=rows_for(0))

    def packed(row):
        cells = sea_rows[pl.ds(row, 1), :]
        base = row & ~3
        lane = spread_rows(cells & (LANES - 1))
        inside = spread_rows((cells >> 7) & 3)
        total = gathered(wave2[strided(8 + base), :], lane)
        for number in range(1, 4):
            total = jnp.where(inside == number, gathered(wave2[strided(8 + base + number), :], lane), total)
        return total

    def unit_row(chunk, device):
        return jnp.clip(units_smem[0, device], 0, ROWS - 1) if chunk == 0 else device * 4

    def forward(chunk, target):
        return pltpu.make_async_remote_copy(
            outgoing.at[chunk, target], incoming.at[chunk, me], send_sem.at[chunk], forward_sem.at[chunk, me >> 4],
            device_id={"comp": target}, device_id_type=MESH)

    def send(chunk, target):
        outgoing[chunk, target] = packed(unit_row(chunk, target))
        forward(chunk, target).start()

    def quarter_step(number):
        substep(wave1, wave2, range(8), 9, origin=quarter_of(me, number) * 64)

    def quarter_sends(number):
        quarter = quarter_of(me, number)

        @pl.loop(0, 16)
        def _(place):
            target = device_in(me, quarter, place)
            ready = (target >= 4) & (target < BLOCKS - 4) if number == 0 else target != me

            @pl.when(ready)
            def _():
                send(1, target)

    quarter_step(0)
    pl.semaphore_wait(barrier, COMPS + 1)
    send_west = pltpu.make_async_remote_copy(
        to_west, from_east, halo_send.at[0], halo_recv.at[0], device_id={"region": west}, device_id_type=MESH)
    send_east = pltpu.make_async_remote_copy(
        to_east, from_west, halo_send.at[1], halo_recv.at[1], device_id={"region": east}, device_id_type=MESH)
    send_west.start()
    send_east.start()

    quarter_sends(0)

    def prepare(number):
        quarter_mask(number)

        @pl.loop(0, LOCAL, unroll=3)
        def _(comp):
            masked(comp, rows_for(number), 80)

        substep(wave0, wave1, range(10), 9, origin=rows_for(number))

    prepare(1)
    load_kernel.start()
    load_constants.start()
    load_wind.start()

    load_own.wait()
    coefficients = own[...]
    wide = lax.broadcasted_iota(jnp.int32, (LOCAL, LANES), 1)

    def column(number):
        return spread_rows(coefficients[:, number : number + 1])

    centre_w, west_w, east_w = column(3), column(4), column(5)
    south_w = jnp.where(wide == 0, 0.0, column(6))
    north_w = jnp.where(wide == LANES - 1, 0.0, column(7))

    def halo(rows, inside, outermost, before):
        near = jnp.where(inside, rows[0], 0.0)
        far = jnp.where(inside, rows[1], 0.0)
        sides = (far, outermost) if before else (outermost, far)
        changed = (
            centre_w * near + west_w * sides[0] + east_w * sides[1]
            + south_w * pltpu.roll(near, 1, 1) + north_w * pltpu.roll(near, LANES - 1, 1)
        )
        at = strided(7 if before else 8 + ROWS)
        wave0[at, :] = near
        wave1[at, :] = rows[2] * changed

    send_west.wait()
    send_east.wait()
    halo(from_west, region > 0, first_row, True)
    halo(from_east, region < REGIONS - 1, last_row, False)
    substep(wave0, wave1, (0, ROWS // 8 - 1), 9)
    substep(wave1, wave2, (0, ROWS // 8 - 1), 9)
    quarter_step(1)
    quarter_sends(1)

    row_number = lax.broadcasted_iota(jnp.int32, (ROWS, LANES), 0)
    lane_position = lax.broadcasted_iota(jnp.int32, (ROWS, LANES), 1)
    later = (sea_rows[0:ROWS, :] >= 0) & ((row_number & 3) > 0)
    count = jnp.where(later, 1.0, 0.0)
    lower = jnp.where(
        lax.broadcasted_iota(jnp.int32, (ROWS, ROWS), 0) > lax.broadcasted_iota(jnp.int32, (ROWS, ROWS), 1), 1.0, 0.0
    ).astype(jnp.bfloat16)
    rank = jnp.dot(lower, count.astype(jnp.bfloat16), preferred_element_type=F32)
    found = jnp.where((rank == lane_position.astype(F32)) & later, row_number.astype(F32), 0.0)
    before = jnp.where(row_number < lane_position * 4, count, 0.0)
    unit_rows = jnp.broadcast_to(jnp.sum(found, axis=0, keepdims=True), (4, LANES))
    first_units = jnp.broadcast_to(jnp.sum(before, axis=0, keepdims=True), (4, LANES))
    units[...] = jnp.concatenate([unit_rows, first_units], axis=0).astype(jnp.int32)
    load_units = pltpu.make_async_copy(units, units_smem, load_sem.at[5])
    load_units.start()

    prepare(2)
    quarter_step(2)
    quarter_sends(2)
    prepare(3)
    quarter_step(3)
    quarter_sends(3)

    @pl.when((first_quarter == 0) | (first_quarter == 3))
    def _():
        @pl.loop(0, 4)
        def _(place):
            send(1, first_quarter * 20 + ((me + place) & 3))

    load_units.wait()

    @pl.loop(0, 4)
    def _(number):
        quarter = quarter_of(me, number)

        @pl.loop(0, 16)
        def _(place):
            target = device_in(me, quarter, place)

            @pl.when(target != me)
            def _():
                send(0, target)

    for chunk in range(2):
        incoming[chunk, me] = packed(unit_row(chunk, me))

    load_constants.wait()

    @pl.loop(0, COMPS, unroll=4)
    def _(source):
        values = constants[source]
        omega[source] = spread_rows(values[:, 0:1])
        cosine[source] = spread_rows(values[:, 1:2])
        sine[source] = spread_rows(values[:, 2:3])

    slot = lax.broadcasted_iota(jnp.int32, (1, 4 * LANES), 1)
    slot_lane = (slot & (LANES - 1)).astype(F32)
    slot_part = (slot >> 7).astype(F32)

    @pl.loop(0, BLOCKS, unroll=8)
    def _(block):
        maps = listed_maps(block, [slot_lane, slot_part])
        rows = block_rows(block)
        lane_map[rows, :] = maps[0:4].astype(jnp.int32)
        part_map[rows, :] = jnp.where(mask[rows, :] > 0.5, maps[8:12], -1.0).astype(jnp.int32)

    load_kernel.wait()
    load_wind.wait()

    def wind_at(row):
        cells = sea_rows[pl.ds(row, 1), :]
        base = row & ~3
        lane = jnp.broadcast_to(cells & (LANES - 1), (8, LANES))
        inside = (cells >> 7) & 3
        parts = []
        for part in range(2):
            total = jnp.zeros((8, LANES), F32)
            for number in range(4):
                line = jnp.broadcast_to(wind[pl.ds(part * ROWS + base + number, 1), :], (8, LANES))
                total = jnp.where(inside == number, gathered(line, lane), total)
            parts.append(total[0:1])
        return parts

    def back(chunk, target, held):
        return pltpu.make_async_remote_copy(
            returning.at[chunk, target], held.at[me], send_sem.at[2 + chunk], back_sem.at[chunk, me >> 3],
            device_id={"comp": target}, device_id_type=MESH)

    def source_terms(chunk, held):
        wind_u, wind_v = wind_at(unit_row(chunk, me))
        total = jnp.zeros((LOCAL, LANES), F32)
        for number, turn in enumerate((2, 1, 3, 0)):
            quarter = ((me >> 4) + 4 - turn) & 3
            landed = incoming.at[chunk, pl.ds(0, 16 if number < 3 else 15)]
            pltpu.make_async_copy(landed, landed, forward_sem.at[chunk, quarter]).wait()
            start = pl.multiple_of(quarter * TILE, TILE)
            for place in range(16):
                values = incoming[chunk, quarter * 16 + place]
                dense[pl.ds(start + place * LOCAL, LOCAL), :] = values
                total = total + omega[quarter * 16 + place] * values
            rounded[pl.ds(start, TILE), :] = dense[pl.ds(start, TILE), :].astype(jnp.bfloat16)

        energy = jnp.sum(total, axis=0, keepdims=True) * energy_scale()
        loss = dissipation * energy * energy

        def updated(target):
            points = incoming[chunk, target]
            speed = omega[target]
            along = cosine[target] * wind_u + sine[target] * wind_v
            growth = growth_rate * speed * jnp.maximum(along - wind_floor, 0.0)
            damping = speed * speed * loss
            joined = coupled[pl.ds(target * LOCAL, LOCAL), :]
            return points + points * (growth - damping + coupling * joined) / (1.0 + damping)

        def update(number, sending):
            quarter = quarter_of(me, number)
            rows = pl.ds(pl.multiple_of(quarter * TILE, TILE), TILE)
            coupled[rows, :] = jnp.dot(kernel_buf[rows, :], rounded[...], preferred_element_type=F32)

            @pl.loop(0, 16, unroll=4)
            def _(place):
                target = device_in(me, quarter, place)
                values = updated(target)
                returning[chunk, target] = values

                @pl.when(target == me)
                def _():
                    held[me] = values

                if sending:

                    @pl.when(target != me)
                    def _():
                        back(chunk, target, held).start()

        return update

    update = source_terms(1, arrived_b)

    @pl.loop(0, EARLY)
    def _(number):
        update(number, True)

    @pl.loop(EARLY, 4)
    def _(number):
        update(number, False)

    update_later = source_terms(0, arrived_a)

    @pl.loop(0, 4)
    def _(number):
        update_later(number, True)

    @pl.loop(EARLY, 4)
    def _(number):
        quarter = quarter_of(me, number)

        @pl.loop(0, 16)
        def _(place):
            target = device_in(me, quarter, place)

            @pl.when(target != me)
            def _():
                back(1, target, arrived_b).start()

    def plane_of(number):
        shift = (4, 4, 2, 2, 6, 6, 0, 0)[number]
        return (((me >> 3) + 8 - shift) & 6) + (((me >> 3) + number + 1) & 1)

    def arrival(number, chunk, held):
        landed = held.at[pl.ds(0, 8 if number < 7 else 7)]
        pltpu.make_async_copy(landed, landed, back_sem.at[chunk, plane_of(number)]).wait()

    for number in range(8):
        arrival(number, 0, arrived_a)

        @pl.loop(0, 8, unroll=4)
        def _(place, number=number):
            unit = plane_of(number) * 8 + place
            base = jnp.clip(units_smem[0, unit], 0, ROWS - 1) & ~3
            values = arrived_a[unit]
            for line in range(4):
                lane = spread_rows(lane_map[pl.ds(base + line, 1), :])
                expanded[unit * 4 + line] = gathered(values, lane)

    def finish(block):
        values = arrived_b[block]
        first_unit = units_smem[4, block]
        for number in range(4):
            x = block * 4 + number
            line = pl.ds(x, 1)
            lane, part = spread_rows(lane_map[line, :]), spread_rows(part_map[line, :])
            piece = jnp.where(part == 0, gathered(values, lane), 0.0)
            for offset in range(3):
                unit = jnp.clip(first_unit + offset, 0, COMPS - 1)
                piece = jnp.where(part == offset + 1, expanded[unit * 4 + number], piece)
            result[pl.ds(x, LOCAL, stride=ROWS), :] = piece

    for number in range(8):
        arrival(number, 1, arrived_b)

        @pl.loop(0, 8, unroll=4)
        def _(place, number=number):
            finish(plane_of(number) * 8 + place)

    for number in range(4):
        sent = outgoing.at[0, pl.ds(0, COMPS - 1)]
        pltpu.make_async_copy(sent, sent, send_sem.at[number]).wait()


def on_device(spectrum, wind, sea_table, transfer_kernel):
    table, scalars = (jnp.asarray(array) for array in component_tables())
    anywhere = pl.BlockSpec(memory_space=pltpu.HBM)
    wave = pltpu.VMEM((PADDED_COMP * STRIDE, LANES), F32)
    line_map = pltpu.VMEM((PADDED_ROWS, LANES), jnp.int32)
    per_source = pltpu.VMEM((COMPS, LOCAL, LANES), F32)
    per_chunk = pltpu.VMEM((2, COMPS, LOCAL, LANES), F32)
    rim = pltpu.VMEM((3, LOCAL, LANES), F32)
    dense = pltpu.VMEM((PADDED_SPEC, LANES), F32)
    dma = pltpu.SemaphoreType.DMA
    result = pl.pallas_call(
        exchange_kernel,
        out_shape=pltpu.VMEM((PADDED_COMP * ROWS, LANES), F32),
        in_specs=[anywhere] * 6,
        out_specs=pl.BlockSpec(memory_space=pltpu.VMEM),
        scratch_shapes=[
            wave,
            wave,
            wave,
            pltpu.VMEM((BLOCKS, 4 * LANES), jnp.int32),
            pltpu.VMEM((PADDED_ROWS, LANES), F32),
            line_map,
            line_map,
            line_map,
            pltpu.VMEM((8, LANES), jnp.int32),
            pltpu.SMEM((8, LANES), jnp.int32),
            pltpu.SMEM((8, LANES), F32),
            pltpu.VMEM((2 * ROWS + 8, LANES), F32),
            pltpu.VMEM((SPEC, SPEC), jnp.bfloat16),
            per_source,
            pltpu.VMEM((LOCAL, LANES), F32),
            per_source,
            per_source,
            per_source,
            rim,
            rim,
            rim,
            rim,
            per_chunk,
            per_chunk,
            dense,
            pltpu.VMEM((SPEC, LANES), jnp.bfloat16),
            dense,
            per_chunk,
            per_source,
            per_source,
            pltpu.VMEM((ROWS, LOCAL, LANES), F32),
            dma((7,)),
            dma((LOCAL // SHARE,)),
            dma((2,)),
            dma((2,)),
            dma((4,)),
            dma((2, 4)),
            dma((2, 8)),
        ],
        compiler_params=pltpu.CompilerParams(
            collective_id=0, has_side_effects=True, vmem_limit_bytes=59 * 1024 * 1024
        ),
        cost_estimate=pl.CostEstimate(flops=2 * SPEC * SPEC * 256, bytes_accessed=16 << 20, transcendentals=0),
        name="exchange",
    )(spectrum, wind.reshape(2 * ROWS, LANES), sea_table, transfer_kernel, table, scalars)
    return result[: LOCAL * ROWS].reshape(LOCAL, ROWS, LANES)


def solution(mesh):
    placed = (P("comp", "region", None), P(None, "region", None), P("region", None), P())
    return jax.shard_map(
        on_device, mesh=mesh, in_specs=placed, out_specs=P("comp", "region", None), check_vma=False
    )
```

```python
import math

import jax
import jax.numpy as jnp
import numpy as np
from jax import lax
from jax.experimental import pallas as pl
from jax.experimental.pallas import tpu as pltpu
from jax.sharding import PartitionSpec as P

NDIR = 36
NFREQ = 48
SPEC = NDIR * NFREQ
COMPS = 64
LOCAL = SPEC // COMPS
REGIONS = 4
ROWS = 256
LANES = 128
BLOCKS = 64
STRIDE = ROWS + 16
PADDED_ROWS = ROWS + 8
PADDED_COMP = 32
PADDED_SPEC = SPEC + 32
TILE = 432
EARLY = 1
SHARE = 9
F32 = jnp.float32
MESH = pl.DeviceIdType.MESH

growth_rate = 0.05
wind_floor = 0.5
dissipation = 0.02
coupling = 0.5
courant_top = 0.6


def component_tables():
    comp = np.arange(SPEC)
    freq, direction = comp // NDIR, 2.0 * math.pi * (comp % NDIR + 0.5) / NDIR
    omega = 1.1 ** (freq - NFREQ // 2)
    speed = courant_top * 1.1 ** (-freq.astype(np.float64))
    cosine, sine = np.cos(direction), np.sin(direction)
    u, v = speed * cosine, speed * sine
    centre = 1.0 - np.abs(u) - np.abs(v)
    columns = [omega, cosine, sine, centre, np.maximum(u, 0), np.maximum(-u, 0), np.maximum(v, 0), np.maximum(-v, 0)]
    table = np.zeros((SPEC, LANES), np.float32)
    for lane, column in enumerate(columns):
        table[:, lane] = column
    scalars = np.zeros((COMPS, 8, LANES), np.float32)
    for row, column in enumerate([centre, np.abs(u), np.abs(v)]):
        scalars[:, row, :LOCAL] = column.reshape(COMPS, LOCAL)
    return table.reshape(COMPS, LOCAL, LANES), scalars


def energy_scale():
    return float(1.0 / (NDIR * np.sum(1.1 ** (np.arange(NFREQ) - NFREQ // 2.0))))


def shifted(me, step):
    z = ((me & 56) + (step & 56)) & 56
    y = ((me & 6) + (step & 6)) & 6
    return z + y + ((me + step) & 1)


def quarter_of(me, number):
    order = jnp.where(number == 2, 3, jnp.where(number == 3, 0, 2 - number))
    return ((me >> 4) + order) & 3


def device_in(me, quarter, place):
    return quarter * 16 + ((me ^ place ^ 8) & 8) + ((me + place) & 7)


def gathered(source, lanes):
    return jnp.take_along_axis(source, lanes, axis=1, mode="promise_in_bounds")


def spread_rows(row):
    return jnp.broadcast_to(row, (LOCAL, LANES))


def exchange_kernel(
    spectrum, wind_field, listed, transfer, table, scalars,
    result,
    wave0, wave1, wave2, sea_table, mask, sea_rows, lane_map, part_map, units, units_smem, scalars_smem,
    wind, kernel_buf, constants, own, omega, cosine, sine,
    to_west, to_east, from_west, from_east,
    outgoing, incoming, dense, rounded, coupled, returning, arrived_a, arrived_b, expanded,
    load_sem, comp_sem, halo_send, halo_recv, send_sem, forward_sem, back_sem,
):
    me = lax.axis_index("comp")
    region = lax.axis_index("region")
    west = (region + REGIONS - 1) & (REGIONS - 1)
    east = (region + 1) & (REGIONS - 1)

    def comp_load(comp):
        return pltpu.make_async_copy(
            spectrum.at[comp], wave0.at[pl.ds(comp * STRIDE + 8, ROWS)], comp_sem.at[comp // SHARE])

    barrier = pltpu.get_barrier_semaphore()

    for step in range(1, COMPS):
        pl.semaphore_signal(barrier, inc=1, device_id={"comp": shifted(me, step)}, device_id_type=MESH)
    pl.semaphore_signal(barrier, inc=1, device_id={"region": west}, device_id_type=MESH)
    pl.semaphore_signal(barrier, inc=1, device_id={"region": east}, device_id_type=MESH)

    load_listed = pltpu.make_async_copy(listed, sea_table, load_sem.at[6])
    load_listed.start()

    for comp in range(LOCAL):
        comp_load(comp).start()

    load_scalars = pltpu.make_async_copy(scalars.at[me], scalars_smem, load_sem.at[0])
    load_scalars.start()
    load_own = pltpu.make_async_copy(table.at[me], own, load_sem.at[1])
    load_own.start()
    load_constants = pltpu.make_async_copy(table, constants, load_sem.at[2])
    load_kernel = pltpu.make_async_copy(transfer, kernel_buf, load_sem.at[3])
    load_wind = pltpu.make_async_copy(wind_field, wind.at[pl.ds(0, 2 * ROWS)], load_sem.at[4])
    load_listed.wait()

    for part in range(4):
        sea_rows[pl.ds(part, BLOCKS, stride=4), :] = sea_table[:, part * LANES : (part + 1) * LANES]

    lane_number = lax.broadcasted_iota(jnp.int32, (LANES, 4 * LANES), 0)
    quarter = lax.broadcasted_iota(jnp.int32, (8, 4 * LANES), 0)

    def listed_maps(block, weights):
        cells = sea_table[pl.ds(block, 1), :]
        lane = jnp.where(cells >= 0, cells & (LANES - 1), -1)
        inside = jnp.where(cells >= 0, (cells >> 7) & 3, -1)
        match = jnp.where(lane == lane_number, 1.0, 0.0).astype(jnp.bfloat16)
        row = jnp.where(inside == quarter, 1.0, 0.0)
        rows = jnp.concatenate([row * w for w in weights], axis=0).astype(jnp.bfloat16)
        return lax.dot_general(rows, match, (((1,), (1,)), ((), ())), preferred_element_type=F32)

    def block_rows(block):
        return pl.ds(pl.multiple_of(block * 4, 4), 4)

    def mask_block(block):
        mask[block_rows(block), :] = listed_maps(block, [1.0])[0:4]

    def strided(x):
        return pl.ds(x, LOCAL, stride=STRIDE)

    def masked(comp, start, count):
        rows = pl.ds(pl.multiple_of(comp * STRIDE + 8 + start, 8), count)
        wave0[rows, :] = mask[pl.ds(pl.multiple_of(start, 8), count), :] * wave0[rows, :]

    first_quarter = quarter_of(me, 0)

    def rows_for(number):
        return jnp.clip(quarter_of(me, number) * 64 - 8, 0, ROWS - 80)

    def quarter_mask(number):
        @pl.loop(0, 20, unroll=10)
        def _(place):
            mask_block((rows_for(number) >> 2) + place)

    quarter_mask(0)
    for block in (0, 1, BLOCKS - 2, BLOCKS - 1):
        mask_block(block)

    for share in range(LOCAL // SHARE):
        landed = wave0.at[pl.ds(0, SHARE * ROWS)]
        pltpu.make_async_copy(landed, landed, comp_sem.at[share]).wait()

        @pl.loop(share * SHARE, (share + 1) * SHARE, unroll=3)
        def _(comp):
            masked(comp, rows_for(0), 80)
            masked(comp, 0, 8)
            masked(comp, ROWS - 8, 8)

    nothing = jnp.zeros((LOCAL, LANES), F32)
    for wave in (wave0, wave1):
        wave[strided(7), :] = nothing
        wave[strided(8 + ROWS), :] = nothing

    first_row, last_row = wave0[strided(8), :], wave0[strided(7 + ROWS), :]
    to_west[0] = first_row
    to_west[1] = wave0[strided(9), :]
    to_west[2] = spread_rows(mask[0:1, :])
    to_east[0] = last_row
    to_east[1] = wave0[strided(6 + ROWS), :]
    to_east[2] = spread_rows(mask[ROWS - 1 : ROWS, :])
    load_scalars.wait()
    lanes = lax.broadcasted_iota(jnp.int32, (8, LANES), 1)

    def substep(source, target, groups, unroll, origin=0):
        @pl.loop(0, LOCAL, unroll=unroll)
        def _(comp):
            direction = lax.rem(me * LOCAL + comp, NDIR)
            aside = jnp.where((direction < NDIR // 4) | (direction >= 3 * NDIR // 4), -1, 1)
            turn = jnp.where(direction < NDIR // 2, 1, LANES - 1)
            edge = jnp.where(direction < NDIR // 2, 0, LANES - 1)
            centre_w = jnp.full((8, LANES), scalars_smem[0, comp])
            x_w = jnp.full((8, LANES), scalars_smem[1, comp])
            y_w = jnp.where(lanes == edge, 0.0, scalars_smem[2, comp])
            for group in groups:
                row = pl.multiple_of(origin + 8 * group, 8)
                base = pl.multiple_of(comp * STRIDE + 8 + row, 8)
                here = source[pl.ds(base, 8), :]
                beside = source[pl.ds(base + aside, 8), :]
                changed = centre_w * here + x_w * beside + y_w * pltpu.roll(here, turn, 1)
                target[pl.ds(base, 8), :] = mask[pl.ds(row, 8), :] * changed

    substep(wave0, wave1, range(10), 9, origin=rows_for(0))

    def packed(row):
        cells = sea_rows[pl.ds(row, 1), :]
        base = row & ~3
        lane = spread_rows(cells & (LANES - 1))
        inside = spread_rows((cells >> 7) & 3)
        total = gathered(wave2[strided(8 + base), :], lane)
        for number in range(1, 4):
            total = jnp.where(inside == number, gathered(wave2[strided(8 + base + number), :], lane), total)
        return total

    def unit_row(chunk, device):
        return jnp.clip(units_smem[0, device], 0, ROWS - 1) if chunk == 0 else device * 4

    def forward(chunk, target):
        return pltpu.make_async_remote_copy(
            outgoing.at[chunk, target], incoming.at[chunk, me], send_sem.at[chunk], forward_sem.at[chunk, me >> 4],
            device_id={"comp": target}, device_id_type=MESH)

    def send(chunk, target):
        outgoing[chunk, target] = packed(unit_row(chunk, target))
        forward(chunk, target).start()

    def quarter_step(number):
        substep(wave1, wave2, range(8), 9, origin=quarter_of(me, number) * 64)

    def quarter_sends(number):
        quarter = quarter_of(me, number)

        @pl.loop(0, 16)
        def _(place):
            target = device_in(me, quarter, place)
            ready = (target >= 4) & (target < BLOCKS - 4) if number == 0 else target != me

            @pl.when(ready)
            def _():
                send(1, target)

    quarter_step(0)
    pl.semaphore_wait(barrier, COMPS + 1)
    send_west = pltpu.make_async_remote_copy(
        to_west, from_east, halo_send.at[0], halo_recv.at[0], device_id={"region": west}, device_id_type=MESH)
    send_east = pltpu.make_async_remote_copy(
        to_east, from_west, halo_send.at[1], halo_recv.at[1], device_id={"region": east}, device_id_type=MESH)
    send_west.start()
    send_east.start()

    quarter_sends(0)

    def prepare(number):
        quarter_mask(number)

        @pl.loop(0, LOCAL, unroll=3)
        def _(comp):
            masked(comp, rows_for(number), 80)

        substep(wave0, wave1, range(10), 9, origin=rows_for(number))

    prepare(1)
    load_kernel.start()
    load_constants.start()
    load_wind.start()

    load_own.wait()
    coefficients = own[...]
    wide = lax.broadcasted_iota(jnp.int32, (LOCAL, LANES), 1)

    def column(number):
        return spread_rows(coefficients[:, number : number + 1])

    centre_w, west_w, east_w = column(3), column(4), column(5)
    south_w = jnp.where(wide == 0, 0.0, column(6))
    north_w = jnp.where(wide == LANES - 1, 0.0, column(7))

    def halo(rows, inside, outermost, before):
        near = jnp.where(inside, rows[0], 0.0)
        far = jnp.where(inside, rows[1], 0.0)
        sides = (far, outermost) if before else (outermost, far)
        changed = (
            centre_w * near + west_w * sides[0] + east_w * sides[1]
            + south_w * pltpu.roll(near, 1, 1) + north_w * pltpu.roll(near, LANES - 1, 1)
        )
        at = strided(7 if before else 8 + ROWS)
        wave0[at, :] = near
        wave1[at, :] = rows[2] * changed

    send_west.wait()
    send_east.wait()
    halo(from_west, region > 0, first_row, True)
    halo(from_east, region < REGIONS - 1, last_row, False)
    substep(wave0, wave1, (0, ROWS // 8 - 1), 9)
    substep(wave1, wave2, (0, ROWS // 8 - 1), 9)
    quarter_step(1)
    quarter_sends(1)

    row_number = lax.broadcasted_iota(jnp.int32, (ROWS, LANES), 0)
    lane_position = lax.broadcasted_iota(jnp.int32, (ROWS, LANES), 1)
    later = (sea_rows[0:ROWS, :] >= 0) & ((row_number & 3) > 0)
    count = jnp.where(later, 1.0, 0.0)
    lower = jnp.where(
        lax.broadcasted_iota(jnp.int32, (ROWS, ROWS), 0) > lax.broadcasted_iota(jnp.int32, (ROWS, ROWS), 1), 1.0, 0.0
    ).astype(jnp.bfloat16)
    rank = jnp.dot(lower, count.astype(jnp.bfloat16), preferred_element_type=F32)
    found = jnp.where((rank == lane_position.astype(F32)) & later, row_number.astype(F32), 0.0)
    before = jnp.where(row_number < lane_position * 4, count, 0.0)
    unit_rows = jnp.broadcast_to(jnp.sum(found, axis=0, keepdims=True), (4, LANES))
    first_units = jnp.broadcast_to(jnp.sum(before, axis=0, keepdims=True), (4, LANES))
    units[...] = jnp.concatenate([unit_rows, first_units], axis=0).astype(jnp.int32)
    load_units = pltpu.make_async_copy(units, units_smem, load_sem.at[5])
    load_units.start()

    prepare(2)
    quarter_step(2)
    quarter_sends(2)
    prepare(3)
    quarter_step(3)
    quarter_sends(3)

    @pl.when((first_quarter == 0) | (first_quarter == 3))
    def _():
        @pl.loop(0, 4)
        def _(place):
            send(1, first_quarter * 20 + ((me + place) & 3))

    load_units.wait()

    @pl.loop(0, 4)
    def _(number):
        quarter = quarter_of(me, number)

        @pl.loop(0, 16)
        def _(place):
            target = device_in(me, quarter, place)

            @pl.when(target != me)
            def _():
                send(0, target)

    for chunk in range(2):
        incoming[chunk, me] = packed(unit_row(chunk, me))

    load_constants.wait()

    @pl.loop(0, COMPS, unroll=4)
    def _(source):
        values = constants[source]
        omega[source] = spread_rows(values[:, 0:1])
        cosine[source] = spread_rows(values[:, 1:2])
        sine[source] = spread_rows(values[:, 2:3])

    slot = lax.broadcasted_iota(jnp.int32, (1, 4 * LANES), 1)
    slot_lane = (slot & (LANES - 1)).astype(F32)
    slot_part = (slot >> 7).astype(F32)

    @pl.loop(0, BLOCKS, unroll=8)
    def _(block):
        maps = listed_maps(block, [slot_lane, slot_part])
        rows = block_rows(block)
        lane_map[rows, :] = maps[0:4].astype(jnp.int32)
        part_map[rows, :] = jnp.where(mask[rows, :] > 0.5, maps[8:12], -1.0).astype(jnp.int32)

    load_kernel.wait()
    load_wind.wait()

    def wind_at(row):
        cells = sea_rows[pl.ds(row, 1), :]
        base = row & ~3
        lane = jnp.broadcast_to(cells & (LANES - 1), (8, LANES))
        inside = (cells >> 7) & 3
        parts = []
        for part in range(2):
            total = jnp.zeros((8, LANES), F32)
            for number in range(4):
                line = jnp.broadcast_to(wind[pl.ds(part * ROWS + base + number, 1), :], (8, LANES))
                total = jnp.where(inside == number, gathered(line, lane), total)
            parts.append(total[0:1])
        return parts

    def back(chunk, target, held):
        return pltpu.make_async_remote_copy(
            returning.at[chunk, target], held.at[me], send_sem.at[2 + chunk], back_sem.at[chunk, me >> 3],
            device_id={"comp": target}, device_id_type=MESH)

    def source_terms(chunk, held):
        wind_u, wind_v = wind_at(unit_row(chunk, me))
        total = jnp.zeros((LOCAL, LANES), F32)
        for number, turn in enumerate((2, 1, 3, 0)):
            quarter = ((me >> 4) + 4 - turn) & 3
            landed = incoming.at[chunk, pl.ds(0, 16 if number < 3 else 15)]
            pltpu.make_async_copy(landed, landed, forward_sem.at[chunk, quarter]).wait()
            start = pl.multiple_of(quarter * TILE, TILE)
            for place in range(16):
                values = incoming[chunk, quarter * 16 + place]
                dense[pl.ds(start + place * LOCAL, LOCAL), :] = values
                total = total + omega[quarter * 16 + place] * values
            rounded[pl.ds(start, TILE), :] = dense[pl.ds(start, TILE), :].astype(jnp.bfloat16)

        energy = jnp.sum(total, axis=0, keepdims=True) * energy_scale()
        loss = dissipation * energy * energy

        def updated(target):
            points = incoming[chunk, target]
            speed = omega[target]
            along = cosine[target] * wind_u + sine[target] * wind_v
            growth = growth_rate * speed * jnp.maximum(along - wind_floor, 0.0)
            damping = speed * speed * loss
            joined = coupled[pl.ds(target * LOCAL, LOCAL), :]
            return points + points * (growth - damping + coupling * joined) / (1.0 + damping)

        def update(number, sending):
            quarter = quarter_of(me, number)
            rows = pl.ds(pl.multiple_of(quarter * TILE, TILE), TILE)
            coupled[rows, :] = jnp.dot(kernel_buf[rows, :], rounded[...], preferred_element_type=F32)

            @pl.loop(0, 16, unroll=4)
            def _(place):
                target = device_in(me, quarter, place)
                values = updated(target)
                returning[chunk, target] = values

                @pl.when(target == me)
                def _():
                    held[me] = values

                if sending:

                    @pl.when(target != me)
                    def _():
                        back(chunk, target, held).start()

        return update

    update = source_terms(1, arrived_b)

    @pl.loop(0, EARLY)
    def _(number):
        update(number, True)

    @pl.loop(EARLY, 4)
    def _(number):
        update(number, False)

    update_later = source_terms(0, arrived_a)

    @pl.loop(0, 4)
    def _(number):
        update_later(number, True)

    @pl.loop(EARLY, 4)
    def _(number):
        quarter = quarter_of(me, number)

        @pl.loop(0, 16)
        def _(place):
            target = device_in(me, quarter, place)

            @pl.when(target != me)
            def _():
                back(1, target, arrived_b).start()

    def plane_of(number):
        shift = (4, 4, 2, 2, 6, 6, 0, 0)[number]
        return (((me >> 3) + 8 - shift) & 6) + (((me >> 3) + number + 1) & 1)

    def arrival(number, chunk, held):
        landed = held.at[pl.ds(0, 8 if number < 7 else 7)]
        pltpu.make_async_copy(landed, landed, back_sem.at[chunk, plane_of(number)]).wait()

    for number in range(8):
        arrival(number, 0, arrived_a)

        @pl.loop(0, 8, unroll=4)
        def _(place, number=number):
            unit = plane_of(number) * 8 + place
            base = jnp.clip(units_smem[0, unit], 0, ROWS - 1) & ~3
            values = arrived_a[unit]
            for line in range(4):
                lane = spread_rows(lane_map[pl.ds(base + line, 1), :])
                expanded[unit * 4 + line] = gathered(values, lane)

    def finish(block):
        values = arrived_b[block]
        first_unit = units_smem[4, block]
        for number in range(4):
            x = block * 4 + number
            line = pl.ds(x, 1)
            lane, part = spread_rows(lane_map[line, :]), spread_rows(part_map[line, :])
            piece = jnp.where(part == 0, gathered(values, lane), 0.0)
            for offset in range(3):
                unit = jnp.clip(first_unit + offset, 0, COMPS - 1)
                piece = jnp.where(part == offset + 1, expanded[unit * 4 + number], piece)
            result[pl.ds(x, LOCAL, stride=ROWS), :] = piece

    for number in range(8):
        arrival(number, 1, arrived_b)

        @pl.loop(0, 8, unroll=8)
        def _(place, number=number):
            finish(plane_of(number) * 8 + place)

    for number in range(4):
        sent = outgoing.at[0, pl.ds(0, COMPS - 1)]
        pltpu.make_async_copy(sent, sent, send_sem.at[number]).wait()


def on_device(spectrum, wind, sea_table, transfer_kernel):
    table, scalars = (jnp.asarray(array) for array in component_tables())
    anywhere = pl.BlockSpec(memory_space=pltpu.HBM)
    wave = pltpu.VMEM((PADDED_COMP * STRIDE, LANES), F32)
    line_map = pltpu.VMEM((PADDED_ROWS, LANES), jnp.int32)
    per_source = pltpu.VMEM((COMPS, LOCAL, LANES), F32)
    per_chunk = pltpu.VMEM((2, COMPS, LOCAL, LANES), F32)
    rim = pltpu.VMEM((3, LOCAL, LANES), F32)
    dense = pltpu.VMEM((PADDED_SPEC, LANES), F32)
    dma = pltpu.SemaphoreType.DMA
    result = pl.pallas_call(
        exchange_kernel,
        out_shape=pltpu.VMEM((PADDED_COMP * ROWS, LANES), F32),
        in_specs=[anywhere] * 6,
        out_specs=pl.BlockSpec(memory_space=pltpu.VMEM),
        scratch_shapes=[
            wave,
            wave,
            wave,
            pltpu.VMEM((BLOCKS, 4 * LANES), jnp.int32),
            pltpu.VMEM((PADDED_ROWS, LANES), F32),
            line_map,
            line_map,
            line_map,
            pltpu.VMEM((8, LANES), jnp.int32),
            pltpu.SMEM((8, LANES), jnp.int32),
            pltpu.SMEM((8, LANES), F32),
            pltpu.VMEM((2 * ROWS + 8, LANES), F32),
            pltpu.VMEM((SPEC, SPEC), jnp.bfloat16),
            per_source,
            pltpu.VMEM((LOCAL, LANES), F32),
            per_source,
            per_source,
            per_source,
            rim,
            rim,
            rim,
            rim,
            per_chunk,
            per_chunk,
            dense,
            pltpu.VMEM((SPEC, LANES), jnp.bfloat16),
            dense,
            per_chunk,
            per_source,
            per_source,
            pltpu.VMEM((ROWS, LOCAL, LANES), F32),
            dma((7,)),
            dma((LOCAL // SHARE,)),
            dma((2,)),
            dma((2,)),
            dma((4,)),
            dma((2, 4)),
            dma((2, 8)),
        ],
        compiler_params=pltpu.CompilerParams(
            collective_id=0, has_side_effects=True, vmem_limit_bytes=59 * 1024 * 1024
        ),
        cost_estimate=pl.CostEstimate(flops=2 * SPEC * SPEC * 256, bytes_accessed=16 << 20, transcendentals=0),
        name="exchange",
    )(spectrum, wind.reshape(2 * ROWS, LANES), sea_table, transfer_kernel, table, scalars)
    return result[: LOCAL * ROWS].reshape(LOCAL, ROWS, LANES)


def solution(mesh):
    placed = (P("comp", "region", None), P(None, "region", None), P("region", None), P())
    return jax.shard_map(
        on_device, mesh=mesh, in_specs=placed, out_specs=P("comp", "region", None), check_vma=False
    )
```
